32 devices in a mesh: row: 16 (over z, x, core), col: 2 (over y).
Axes of the slice: x: 2, y: 2, z: 4, core: 2. Of those that a mesh axis runs over, the one named last changes fastest.
Arguments:
- hessian: float32 [14336, 14336], P('row', 'col'), may hold values from -1 to 6, as said below
- dense_weight: float32 [14336, 1024], P('col', 'row'), may hold values from -6 to 6
- start_iterate: float32 [14336, 1024], P('col', 'row'), may hold values from -6 to 6
- start_multiplier: float32 [14336, 1024], P('col', 'row'), may hold values from -3 to 3
- keep_mask: int32 [14336, 1024], P('col', 'row'), may hold values 0 or 1
Outputs:
- iterate: float32 [14336, 1024], P('col', 'row')
- projected: float32 [14336, 1024], P('col', 'row')
- multiplier: float32 [14336, 1024], P('col', 'row')
The draws below stay inside these ranges and needn't reach their ends.
Inputs may be any that keep to these rules, and one draw needn't show every extreme that they name: `hessian`: a calibration Hessian: symmetric up to rounding and positive definite.
All inputs are finite; a program needn't handle non-finite values. No bound on the sum of `keep_mask` on one device may be relied on, other than what follows from the above.
Results may differ from the reference program's by a relative error of at most 0.0001.
Values sent between devices are 32-bit elements; how exact they have to be, the bound alone decides.
No kernel may reach another device: no remote copies, remote signals or barrier semaphores. Data moves between devices by JAX's collectives and lax.ppermute only.
A program may use at most 128 MiB of HBM per device.

```python
import math
import jax
import jax.numpy as jnp
from jax import lax

K = 14336
R = 1024
ITERS = 2


def draw_hessian(key, part):
    key_off = jax.random.fold_in(key, 11)
    key_diag = jax.random.fold_in(key, 12)
    key_scale = jax.random.fold_in(key, 13)
    base = jax.random.normal(key_off, (K, K), jnp.float32)
    scales = jnp.exp(jax.random.uniform(key_scale, (K,), jnp.float32, math.log(0.7), math.log(1.4)))
    offdiag = (base + base.T) * (0.25 / math.sqrt(K))
    diagonal = jax.random.uniform(key_diag, (K,), jnp.float32, 1.0, 2.0)
    places = jnp.arange(K)
    core = offdiag.at[places, places].set(diagonal)
    return scales[:, None] * core * scales[None, :]


def set_ends(drawn, key, low, top_value):
    longest = drawn.shape.index(max(drawn.shape))
    spots = []
    for shift in (0, 1):
        where = [jax.random.randint(jax.random.fold_in(key, axis), (), 0, length) for axis, length in enumerate(drawn.shape)]
        where[longest] = (where[longest] + shift) % drawn.shape[longest]
        spots.append(tuple(where))
    return drawn.at[spots[0]].set(low).at[spots[1]].set(top_value)


def levels(key, dims, pieces, smallest, high):
    loudness = 1.0
    for axis_at, blocks in pieces:
        draws = jax.random.uniform(jax.random.fold_in(jax.random.fold_in(key, 6), axis_at), (blocks,), jnp.float32, smallest / len(pieces), high / len(pieces))
        loudness = loudness * jnp.repeat(jnp.exp(draws), dims[axis_at] // blocks).reshape((-1,) + (1,) * (len(dims) - 1 - axis_at))
    return loudness


def gaussian(rng, extent, spread, limit, cuts=(), kind=jnp.bfloat16):
    gain = levels(rng, extent, cuts, -0.22, 0.18) if cuts else 1.0
    result = jax.random.normal(rng, extent, jnp.float32) * spread * gain
    return jnp.minimum(jnp.maximum(result, -limit), limit).astype(kind)


def setup_inputs(seed: int = 0) -> dict:
    key_of = jax.random.split(jax.random.key(seed), 6)
    hessian = draw_hessian(jax.random.fold_in(key_of[5], 71), 0)
    dense_weight = gaussian(key_of[1], (K, R), 1.0, 6.0, ((0, 2), (1, 16)), jnp.float32)
    start_iterate = gaussian(key_of[2], (K, R), 1.0, 6.0, ((0, 2), (1, 16)), jnp.float32)
    start_multiplier = gaussian(key_of[3], (K, R), 0.5, 3.0, ((0, 2), (1, 16)), jnp.float32)
    keep_mask = set_ends((jax.random.randint(key_of[4], (K, R), 0, 2) < 1).astype(jnp.int32), jax.random.fold_in(key_of[4], 1), 0, 1)
    return {"hessian": hessian, "dense_weight": dense_weight, "start_iterate": start_iterate, "start_multiplier": start_multiplier, "keep_mask": keep_mask}


step_size = 0.25
penalty = 1.0


def reference(hessian, dense_weight, start_iterate, start_multiplier, keep_mask):
    keeping = keep_mask.astype(jnp.float32)
    iterate = start_iterate
    multiplier = start_multiplier
    projected = keeping * (iterate + multiplier)
    for rounds in range(ITERS):
        change = iterate - dense_weight
        gradient = jnp.dot(hessian, change, precision=lax.Precision.HIGHEST, preferred_element_type=jnp.float32)
        iterate = iterate - step_size * (gradient + penalty * (iterate - projected + multiplier))
        projected = keeping * (iterate + multiplier)
        multiplier = multiplier + iterate - projected
    return iterate, projected, multiplier
```

```python
import functools

import jax
import jax.numpy as jnp
from jax import lax
from jax.experimental import pallas as pl
from jax.experimental.pallas import tpu as pltpu
from jax.sharding import PartitionSpec as P

step_size = 0.25
penalty = 1.0

CORES = 2
PAIR = 2
VMEM_BYTES = 48 * 1024 * 1024


def split(value):
    high = value.astype(jnp.bfloat16)
    low = (value - high.astype(jnp.float32)).astype(jnp.bfloat16)
    return high, low


def dot_f32(left, right, rows, dims):
    high, low = split(right)
    both = lax.dot_general(left[...], high, dims, preferred_element_type=jnp.float32)
    cross = lax.dot_general(left[:rows], low, dims, preferred_element_type=jnp.float32)
    return both[:rows] + (both[rows:] + cross)


def first_kernel(near_ref, far_ref, own_ref, sib_ref, xnear_ref, xfar_ref, out_ref, parts):
    half = near_ref.shape[0]
    rows = 2 * half

    @pl.when(pl.program_id(0) == 0)
    def _():
        parts[:half], parts[rows : rows + half] = split(near_ref[...])
        parts[half:rows], parts[rows + half :] = split(far_ref[...])

    tile = own_ref.shape[0]
    rows_of_h = jnp.concatenate([own_ref[...], sib_ref[...]], axis=0)
    product = dot_f32(parts, rows_of_h, rows, (((1,), (1,)), ((), ())))
    for which in range(2):
        part = product[:, which * tile : (which + 1) * tile]
        out_ref[which, :half] = xnear_ref[which] - step_size * part[:half]
        out_ref[which, half:] = xfar_ref[which] - step_size * part[half:]


def first(near, far, own, sib, xnear, xfar):
    half, depth = near.shape
    rows = own.shape[0]
    tile = 128 if rows % 128 == 0 else rows
    whole = pl.BlockSpec((half, depth), lambda i: (0, 0))
    band = pl.BlockSpec((tile, depth), lambda i: (i, 0))
    piece = pl.BlockSpec((2, half, tile), lambda i: (0, 0, i))
    return pl.pallas_call(
        first_kernel,
        grid=(rows // tile,),
        in_specs=[whole, whole, band, band, piece, piece],
        out_specs=pl.BlockSpec((2, 2 * half, tile), lambda i: (0, 0, i)),
        out_shape=jax.ShapeDtypeStruct((2, 2 * half, rows), jnp.float32),
        scratch_shapes=[pltpu.VMEM((4 * half, depth), jnp.bfloat16)],
        compiler_params=pltpu.CompilerParams(vmem_limit_bytes=VMEM_BYTES),
        cost_estimate=pl.CostEstimate(
            flops=3 * 2 * 4 * half * depth * rows, bytes_accessed=8 * rows * depth, transcendentals=0
        ),
        name="first_product",
    )(near, far, own, sib, xnear, xfar)


def second_kernel(mine_ref, other_ref, own_ref, sib_ref, near_ref, far_ref, cnear_ref, cfar_ref, parts):
    _, rows, depth = mine_ref.shape
    half = rows // 2

    @pl.when(pl.program_id(0) == 0)
    def _():
        for which in range(2):
            change = mine_ref[which] + other_ref[which]
            cnear_ref[which] = change[:half]
            cfar_ref[which] = change[half:]
            places = slice(which * depth, (which + 1) * depth)
            parts[:rows, places], parts[rows:, places] = split(change)

    rows_of_h = jnp.concatenate([own_ref[...], sib_ref[...]], axis=0)
    product = dot_f32(parts, rows_of_h, rows, (((1,), (0,)), ((), ())))
    near_ref[...] = product[:half]
    far_ref[...] = product[half:]


def second(mine, other, own, sib):
    _, rows, depth = mine.shape
    half = rows // 2
    columns = own.shape[1]
    tile = next((t for t in (512, 256, 128) if columns % t == 0), columns)
    whole = pl.BlockSpec((2, rows, depth), lambda i: (0, 0, 0))
    band = pl.BlockSpec((depth, tile), lambda i: (0, i))
    out = pl.BlockSpec((half, tile), lambda i: (0, i))
    kept = pl.BlockSpec((2, half, depth), lambda i: (0, 0, 0))
    f32 = jnp.float32
    return pl.pallas_call(
        second_kernel,
        grid=(columns // tile,),
        in_specs=[whole, whole, band, band],
        out_specs=[out, out, kept, kept],
        out_shape=[jax.ShapeDtypeStruct((half, columns), f32)] * 2 + [jax.ShapeDtypeStruct((2, half, depth), f32)] * 2,
        scratch_shapes=[pltpu.VMEM((2 * rows, 2 * depth), jnp.bfloat16)],
        compiler_params=pltpu.CompilerParams(vmem_limit_bytes=VMEM_BYTES),
        cost_estimate=pl.CostEstimate(
            flops=3 * 2 * 2 * rows * depth * columns, bytes_accessed=8 * depth * columns, transcendentals=0
        ),
        name="second_product",
    )(mine, other, own, sib)


def per_device(rows_of, planes, hessian, dense_weight, start_iterate, start_multiplier, keep_mask):
    ring = rows_of // (CORES * PAIR)
    chips = ring * PAIR
    per_plane = chips // planes
    depth, columns = hessian.shape
    half = dense_weight.shape[1]
    row = lax.axis_index("row")
    plane = lax.axis_index("col")
    core = row % CORES
    pair = (row // CORES) % PAIR
    place = row // (CORES * PAIR)

    def device(z, x, c):
        return ((z % ring) * PAIR + x) * CORES + c

    everyone = [(z, x, c) for z in range(ring) for x in range(PAIR) for c in range(CORES)]
    to_sibling = [(device(z, x, c), device(z, x, 1 - c)) for z, x, c in everyone]
    to_pair = [(device(z, x, c), device(z, x ^ 1, c)) for z, x, c in everyone]
    to_next = [(device(z, x, c), device(z + 1, x, c)) for z, x, c in everyone]

    def route(shift, flip):
        pairs = []
        for z, x, c in everyone:
            for y in range(planes):
                chip = ((z + shift) % ring) * PAIR + (x ^ flip)
                if chip // per_plane == y:
                    pairs.append((device(z, x, c) * planes + y, device(z + shift, x ^ flip, c) * planes + y))
        return pairs

    both = ("row", "col")
    permute = lax.ppermute

    keeping = keep_mask.astype(jnp.float32)
    projected = keeping * (start_iterate + start_multiplier)
    change = (start_iterate - dense_weight).T
    sibling = permute(hessian, "row", to_sibling)

    rest = start_iterate - step_size * (penalty * (start_iterate - projected + start_multiplier)) - dense_weight
    rest = rest.reshape(per_plane, CORES, depth, half)
    rest = jnp.where(core == 0, rest, rest[:, ::-1])
    rest = rest.transpose(0, 1, 3, 2)

    def piece(shift, flip):
        chip = ((place + shift) % ring) * PAIR + (pair ^ flip)
        part = lax.dynamic_index_in_dim(rest, jnp.clip(chip - plane * per_plane, 0, per_plane - 1), 0, keepdims=False)
        if shift == 0 and flip == 0:
            return jnp.where(chip // per_plane == plane, part, 0.0)
        return permute(part, both, route(shift, flip))

    def sum_planes(part):
        others = [permute(part, "col", [(y, (y + turn) % planes) for y in range(planes)]) for turn in range(1, planes)]
        return functools.reduce(jnp.add, others) if others else jnp.zeros_like(part)

    near, far, added = {0: change}, {}, {(0, 0): piece(0, 0)}
    mine, other, kept, sent, changed, swapped, back = {}, {}, {}, {}, {}, {}, {}
    total = None
    start = max(ring, 4)
    for window in range(start + ring):
        fresh = []

        def put(where, key, value):
            where[key] = value
            fresh.append((where, key))

        if window == 0:
            put(added, (0, 1), piece(0, 1))
            sibling = permute(hessian, "row", to_sibling)
        if window < ring - 1:
            put(near, window + 1, permute(near[window], "row", to_next))
        if window < ring:
            put(far, window, permute(near[window], "row", to_pair))
        if window < ring - 1:
            for flip in range(PAIR):
                put(added, (window + 1, flip), piece(window + 1, flip))
        group = window - start + 1
        if group >= 1:
            if total is not None:
                total = permute(total, "row", to_next)
            put(swapped, group % ring, permute(sent[group % ring], "row", to_pair))
        group = window - 3
        if 0 <= group < ring:
            for flip in range(PAIR):
                part = changed[group][flip]
                if group or flip:
                    part = permute(part, both, [(b, a) for a, b in route(group, flip)])
                put(back, (group, flip), part)
        group = window - 1
        if 0 <= group < ring:
            put(mine, group, first(near[group], far[group], hessian, sibling, added[group, 0], added[group, 1]))
            put(other, group, sum_planes(mine[group]))
        group = window - 2
        if 0 <= group < ring:
            keep, send, cnear, cfar = second(mine[group], other[group], hessian, sibling)
            put(kept, group, keep)
            put(sent, group, send)
            changed[group] = (cnear, cfar)
        group = window - start + 1
        values = [where[key] for where, key in fresh]
        values, sibling, total = lax.optimization_barrier((values, sibling, total))
        for (where, key), value in zip(fresh, values):
            where[key] = value
        if group >= 1:
            part = kept[group % ring] + swapped[group % ring]
            total = part if total is None else total + part

    back = jnp.stack([back[shift, flip] for shift in range(ring) for flip in range(PAIR)])
    blocks = []
    for block in range(per_plane):
        chip = plane * per_plane + block
        slot = ((chip // PAIR - place) % ring) * PAIR + ((chip % PAIR) ^ pair)
        blocks.append(lax.dynamic_index_in_dim(back, slot, 0, keepdims=False))
    blocks = jnp.stack(blocks)
    blocks = jnp.where(core == 0, blocks, blocks[:, ::-1])
    iterate = blocks.transpose(0, 1, 3, 2).reshape(columns, half) + dense_weight

    projected = keeping * (iterate + start_multiplier)
    multiplier = start_multiplier + iterate - projected
    iterate = iterate - step_size * (total.T + penalty * (iterate - projected + multiplier))
    projected = keeping * (iterate + multiplier)
    multiplier = multiplier + iterate - projected
    return (iterate, projected, multiplier)


def solution(mesh):
    return jax.shard_map(
        functools.partial(per_device, mesh.shape["row"], mesh.shape["col"]),
        mesh=mesh,
        in_specs=(
            P("row", "col"),
            P("col", "row"),
            P("col", "row"),
            P("col", "row"),
            P("col", "row"),
        ),
        out_specs=(P("col", "row"), P("col", "row"), P("col", "row")),
        check_vma=False,
    )
```

```python
import functools

import jax
import jax.numpy as jnp
from jax import lax
from jax.experimental import pallas as pl
from jax.experimental.pallas import tpu as pltpu
from jax.sharding import PartitionSpec as P

step_size = 0.25
penalty = 1.0

CORES = 2
PAIR = 2
VMEM_BYTES = 48 * 1024 * 1024


def split(value):
    high = value.astype(jnp.bfloat16)
    low = (value - high.astype(jnp.float32)).astype(jnp.bfloat16)
    return high, low


def dot_f32(left, right, rows, dims):
    high, low = split(right)
    both = lax.dot_general(left[...], high, dims, preferred_element_type=jnp.float32)
    cross = lax.dot_general(left[:rows], low, dims, preferred_element_type=jnp.float32)
    return both[:rows] + (both[rows:] + cross)


def first_kernel(near_ref, far_ref, own_ref, sib_ref, xnear_ref, xfar_ref, out_ref, parts):
    half = near_ref.shape[0]
    rows = 2 * half

    @pl.when(pl.program_id(0) == 0)
    def _():
        parts[:half], parts[rows : rows + half] = split(near_ref[...])
        parts[half:rows], parts[rows + half :] = split(far_ref[...])

    tile = own_ref.shape[0]
    rows_of_h = jnp.concatenate([own_ref[...], sib_ref[...]], axis=0)
    product = dot_f32(parts, rows_of_h, rows, (((1,), (1,)), ((), ())))
    for which in range(2):
        part = product[:, which * tile : (which + 1) * tile]
        out_ref[which, :half] = xnear_ref[which] - step_size * part[:half]
        out_ref[which, half:] = xfar_ref[which] - step_size * part[half:]


def first(near, far, own, sib, xnear, xfar):
    half, depth = near.shape
    rows = own.shape[0]
    tile = 128 if rows % 128 == 0 else rows
    whole = pl.BlockSpec((half, depth), lambda i: (0, 0))
    band = pl.BlockSpec((tile, depth), lambda i: (i, 0))
    piece = pl.BlockSpec((2, half, tile), lambda i: (0, 0, i))
    return pl.pallas_call(
        first_kernel,
        grid=(rows // tile,),
        in_specs=[whole, whole, band, band, piece, piece],
        out_specs=pl.BlockSpec((2, 2 * half, tile), lambda i: (0, 0, i)),
        out_shape=jax.ShapeDtypeStruct((2, 2 * half, rows), jnp.float32),
        scratch_shapes=[pltpu.VMEM((4 * half, depth), jnp.bfloat16)],
        compiler_params=pltpu.CompilerParams(vmem_limit_bytes=VMEM_BYTES),
        cost_estimate=pl.CostEstimate(
            flops=3 * 2 * 4 * half * depth * rows, bytes_accessed=8 * rows * depth, transcendentals=0
        ),
        name="first_product",
    )(near, far, own, sib, xnear, xfar)


def second_kernel(change_ref, own_ref, sib_ref, near_ref, far_ref, parts):
    _, rows, depth = change_ref.shape
    half = rows // 2

    @pl.when(pl.program_id(0) == 0)
    def _():
        for which in range(2):
            places = slice(which * depth, (which + 1) * depth)
            parts[:rows, places], parts[rows:, places] = split(change_ref[which])

    rows_of_h = jnp.concatenate([own_ref[...], sib_ref[...]], axis=0)
    product = dot_f32(parts, rows_of_h, rows, (((1,), (0,)), ((), ())))
    near_ref[...] = product[:half]
    far_ref[...] = product[half:]


def second(change, own, sib):
    _, rows, depth = change.shape
    half = rows // 2
    columns = own.shape[1]
    tile = next((t for t in (512, 256, 128) if columns % t == 0), columns)
    band = pl.BlockSpec((depth, tile), lambda i: (0, i))
    out = pl.BlockSpec((half, tile), lambda i: (0, i))
    return pl.pallas_call(
        second_kernel,
        grid=(columns // tile,),
        in_specs=[pl.BlockSpec((2, rows, depth), lambda i: (0, 0, 0)), band, band],
        out_specs=[out, out],
        out_shape=[jax.ShapeDtypeStruct((half, columns), jnp.float32)] * 2,
        scratch_shapes=[pltpu.VMEM((2 * rows, 2 * depth), jnp.bfloat16)],
        compiler_params=pltpu.CompilerParams(vmem_limit_bytes=VMEM_BYTES),
        cost_estimate=pl.CostEstimate(
            flops=3 * 2 * 2 * rows * depth * columns, bytes_accessed=8 * depth * columns, transcendentals=0
        ),
        name="second_product",
    )(change, own, sib)


def per_device(rows_of, planes, hessian, dense_weight, start_iterate, start_multiplier, keep_mask):
    ring = rows_of // (CORES * PAIR)
    chips = ring * PAIR
    per_plane = chips // planes
    depth, columns = hessian.shape
    half = dense_weight.shape[1]
    row = lax.axis_index("row")
    plane = lax.axis_index("col")
    core = row % CORES
    pair = (row // CORES) % PAIR
    place = row // (CORES * PAIR)

    def device(z, x, c):
        return ((z % ring) * PAIR + x) * CORES + c

    everyone = [(z, x, c) for z in range(ring) for x in range(PAIR) for c in range(CORES)]
    to_sibling = [(device(z, x, c), device(z, x, 1 - c)) for z, x, c in everyone]
    to_pair = [(device(z, x, c), device(z, x ^ 1, c)) for z, x, c in everyone]
    to_next = [(device(z, x, c), device(z + 1, x, c)) for z, x, c in everyone]

    def route(shift, flip):
        turn = cross(shift, flip)
        pairs = []
        for z, x, c in everyone:
            for y in range(planes):
                chip = ((z + shift) % ring) * PAIR + (x ^ flip)
                if chip // per_plane == (y - turn) % planes:
                    pairs.append((device(z, x, c) * planes + y, device(z + shift, x ^ flip, c) * planes + y))
        return pairs

    def route_back(shift, flip):
        turn = cross(shift, flip)
        return [(b, a - a % planes + (a - turn) % planes) for a, b in route(shift, flip)]

    def cross(shift, flip):
        return 1 if shift and flip else 0

    both = ("row", "col")
    permute = lax.ppermute

    keeping = keep_mask.astype(jnp.float32)
    projected = keeping * (start_iterate + start_multiplier)
    change = (start_iterate - dense_weight).T
    sibling = permute(hessian, "row", to_sibling)

    rest = start_iterate - step_size * (penalty * (start_iterate - projected + start_multiplier)) - dense_weight
    rest = rest.reshape(per_plane, CORES, depth, half)
    rest = jnp.where(core == 0, rest, rest[:, ::-1])
    rest = rest.transpose(0, 1, 3, 2)

    def piece(shift, flip):
        turn = cross(shift, flip)
        chip = ((place + shift) % ring) * PAIR + (pair ^ flip)
        first_chip = ((plane - turn) % planes) * per_plane
        source = rest_by[turn]
        part = lax.dynamic_index_in_dim(source, jnp.clip(chip - first_chip, 0, per_plane - 1), 0, keepdims=False)
        if shift == 0 and flip == 0:
            return jnp.where(chip // per_plane == plane, part, 0.0)
        return permute(part, both, route(shift, flip))

    def sum_planes(part):
        others = [permute(part, "col", [(y, (y + turn) % planes) for y in range(planes)]) for turn in range(1, planes)]
        return functools.reduce(jnp.add, others) if others else jnp.zeros_like(part)

    rest_by = {0: rest}
    near, far, added = {0: change}, {}, {(0, 0): piece(0, 0)}
    mine, other, changed, kept, sent, swapped, back = {}, {}, {}, {}, {}, {}, {}
    total = None
    start = max(ring, 4)
    returns = [(0, 0, 5), (0, 1, 5)] + [(group, flip, group + 2 + (group == 1 and flip)) for group in range(1, ring) for flip in range(PAIR)]
    for window in range(start + ring):
        fresh = []

        def put(where, key, value):
            where[key] = value
            fresh.append((where, key))

        if window < ring - 1:
            put(near, window + 1, permute(near[window], "row", to_next))
        if window < ring:
            put(far, window, permute(near[window], "row", to_pair))
        if window == 0:
            sibling = permute(hessian, "row", to_sibling)
            put(rest_by, 1, permute(rest, "col", [(y, (y + 1) % planes) for y in range(planes)]))
            put(added, (0, 1), piece(0, 1))
        elif window < ring:
            for flip in range(PAIR):
                put(added, (window, flip), piece(window, flip))
        closing = window - start + 1
        if closing >= 1:
            if total is not None:
                total = permute(total, "row", to_next)
            put(swapped, closing % ring, permute(sent[closing % ring], "row", to_pair))
        group = window - 2
        if 0 <= group < ring:
            put(changed, group, mine[group] + other[group])
        group = window - 1
        if 0 <= group < ring:
            put(mine, group, first(near[group], far[group], hessian, sibling, added[group, 0], added[group, 1]))
            put(other, group, sum_planes(mine[group]))
        group = window - 2
        if window == start + ring - 2:
            group = 0
        if (1 <= group < ring) or window == start + ring - 2:
            keep, send = second(changed[group], hessian, sibling)
            put(kept, group, keep)
            put(sent, group, send)
        for group, flip, when in returns:
            if when == window:
                part = changed[group][:, flip * half : (flip + 1) * half]
                if group or flip:
                    part = permute(part, both, route_back(group, flip))
                put(back, (group, flip), part)
        values = [where[key] for where, key in fresh]
        values, sibling, total, rest_by[0] = lax.optimization_barrier((values, sibling, total, rest_by[0]))
        for (where, key), value in zip(fresh, values):
            where[key] = value
        if closing >= 1:
            part = kept[closing % ring] + swapped[closing % ring]
            total = part if total is None else total + part

    back = jnp.stack([back[shift, flip] for shift in range(ring) for flip in range(PAIR)])
    blocks = []
    for block in range(per_plane):
        chip = plane * per_plane + block
        slot = ((chip // PAIR - place) % ring) * PAIR + ((chip % PAIR) ^ pair)
        blocks.append(lax.dynamic_index_in_dim(back, slot, 0, keepdims=False))
    blocks = jnp.stack(blocks)
    blocks = jnp.where(core == 0, blocks, blocks[:, ::-1])
    iterate = blocks.transpose(0, 1, 3, 2).reshape(columns, half) + dense_weight

    projected = keeping * (iterate + start_multiplier)
    multiplier = start_multiplier + iterate - projected
    iterate = iterate - step_size * (total.T + penalty * (iterate - projected + multiplier))
    projected = keeping * (iterate + multiplier)
    multiplier = multiplier + iterate - projected
    return (iterate, projected, multiplier)


def solution(mesh):
    return jax.shard_map(
        functools.partial(per_device, mesh.shape["row"], mesh.shape["col"]),
        mesh=mesh,
        in_specs=(
            P("row", "col"),
            P("col", "row"),
            P("col", "row"),
            P("col", "row"),
            P("col", "row"),
        ),
        out_specs=(P("col", "row"), P("col", "row"), P("col", "row")),
        check_vma=False,
    )
```

```python
import functools

import jax
import jax.numpy as jnp
from jax import lax
from jax.experimental import pallas as pl
from jax.experimental.pallas import tpu as pltpu
from jax.sharding import PartitionSpec as P

step_size = 0.25
penalty = 1.0

CORES = 2
PAIR = 2
VMEM_BYTES = 48 * 1024 * 1024


def split(value):
    high = value.astype(jnp.bfloat16)
    low = (value - high.astype(jnp.float32)).astype(jnp.bfloat16)
    return high, low


def dot_f32(left, right, rows, dims):
    high, low = split(right)
    both = lax.dot_general(left[...], high, dims, preferred_element_type=jnp.float32)
    cross = lax.dot_general(left[:rows], low, dims, preferred_element_type=jnp.float32)
    return both[:rows] + (both[rows:] + cross)


def prepare_kernel(dense_ref, iterate_ref, multiplier_ref, mask_ref, change_ref, rest_ref):
    iterate, multiplier = iterate_ref[...], multiplier_ref[...]
    projected = mask_ref[...].astype(jnp.float32) * (iterate + multiplier)
    change_ref[...] = (iterate - dense_ref[...]).T
    rest_ref[0] = (iterate - step_size * (penalty * (iterate - projected + multiplier)) - dense_ref[...]).T


def prepare(dense, iterate, multiplier, mask, blocks):
    rows, half = dense.shape
    tile = rows // blocks
    band = pl.BlockSpec((tile, half), lambda i: (i, 0))
    return pl.pallas_call(
        prepare_kernel,
        grid=(blocks,),
        in_specs=[band] * 4,
        out_specs=[
            pl.BlockSpec((half, tile), lambda i: (0, i)),
            pl.BlockSpec((1, half, tile), lambda i: (i, 0, 0)),
        ],
        out_shape=[
            jax.ShapeDtypeStruct((half, rows), jnp.float32),
            jax.ShapeDtypeStruct((blocks, half, tile), jnp.float32),
        ],
        compiler_params=pltpu.CompilerParams(vmem_limit_bytes=VMEM_BYTES),
        name="prepare",
    )(dense, iterate, multiplier, mask)


def first_kernel(near_ref, far_ref, own_ref, sib_ref, out_ref, parts):
    half = near_ref.shape[0]
    rows = 2 * half

    @pl.when(pl.program_id(0) == 0)
    def _():
        parts[:half], parts[rows : rows + half] = split(near_ref[...])
        parts[half:rows], parts[rows + half :] = split(far_ref[...])

    tile = own_ref.shape[0]
    rows_of_h = jnp.concatenate([own_ref[...], sib_ref[...]], axis=0)
    product = dot_f32(parts, rows_of_h, rows, (((1,), (1,)), ((), ())))
    for which in range(2):
        out_ref[which] = -step_size * product[:, which * tile : (which + 1) * tile]


def first(near, far, own, sib):
    half, depth = near.shape
    rows = own.shape[0]
    tile = 128 if rows % 128 == 0 else rows
    whole = pl.BlockSpec((half, depth), lambda i: (0, 0))
    band = pl.BlockSpec((tile, depth), lambda i: (i, 0))
    return pl.pallas_call(
        first_kernel,
        grid=(rows // tile,),
        in_specs=[whole, whole, band, band],
        out_specs=pl.BlockSpec((2, 2 * half, tile), lambda i: (0, 0, i)),
        out_shape=jax.ShapeDtypeStruct((2, 2 * half, rows), jnp.float32),
        scratch_shapes=[pltpu.VMEM((4 * half, depth), jnp.bfloat16)],
        compiler_params=pltpu.CompilerParams(vmem_limit_bytes=VMEM_BYTES),
        cost_estimate=pl.CostEstimate(
            flops=3 * 2 * 4 * half * depth * rows, bytes_accessed=8 * rows * depth, transcendentals=0
        ),
        name="first_product",
    )(near, far, own, sib)


def second_kernel(change_ref, own_ref, sib_ref, near_ref, far_ref, parts):
    _, rows, depth = change_ref.shape
    half = rows // 2

    @pl.when(pl.program_id(0) == 0)
    def _():
        for which in range(2):
            places = slice(which * depth, (which + 1) * depth)
            parts[:rows, places], parts[rows:, places] = split(change_ref[which])

    rows_of_h = jnp.concatenate([own_ref[...], sib_ref[...]], axis=0)
    product = dot_f32(parts, rows_of_h, rows, (((1,), (0,)), ((), ())))
    near_ref[...] = product[:half]
    far_ref[...] = product[half:]


def second(change, own, sib):
    _, rows, depth = change.shape
    half = rows // 2
    columns = own.shape[1]
    tile = next((t for t in (512, 256, 128) if columns % t == 0), columns)
    band = pl.BlockSpec((depth, tile), lambda i: (0, i))
    out = pl.BlockSpec((half, tile), lambda i: (0, i))
    return pl.pallas_call(
        second_kernel,
        grid=(columns // tile,),
        in_specs=[pl.BlockSpec((2, rows, depth), lambda i: (0, 0, 0)), band, band],
        out_specs=[out, out],
        out_shape=[jax.ShapeDtypeStruct((half, columns), jnp.float32)] * 2,
        scratch_shapes=[pltpu.VMEM((2 * rows, 2 * depth), jnp.bfloat16)],
        compiler_params=pltpu.CompilerParams(vmem_limit_bytes=VMEM_BYTES),
        cost_estimate=pl.CostEstimate(
            flops=3 * 2 * 2 * rows * depth * columns, bytes_accessed=8 * depth * columns, transcendentals=0
        ),
        name="second_product",
    )(change, own, sib)


def per_device(rows_of, planes, hessian, dense_weight, start_iterate, start_multiplier, keep_mask):
    ring = rows_of // (CORES * PAIR)
    chips = ring * PAIR
    per_plane = chips // planes
    depth, columns = hessian.shape
    half = dense_weight.shape[1]
    row = lax.axis_index("row")
    plane = lax.axis_index("col")
    core = row % CORES
    pair = (row // CORES) % PAIR
    place = row // (CORES * PAIR)

    def device(z, x, c):
        return ((z % ring) * PAIR + x) * CORES + c

    everyone = [(z, x, c) for z in range(ring) for x in range(PAIR) for c in range(CORES)]
    to_sibling = [(device(z, x, c), device(z, x, 1 - c)) for z, x, c in everyone]
    to_pair = [(device(z, x, c), device(z, x ^ 1, c)) for z, x, c in everyone]
    to_next = [(device(z, x, c), device(z + 1, x, c)) for z, x, c in everyone]

    def route(shift, flip):
        turn = cross(shift, flip)
        pairs = []
        for z, x, c in everyone:
            for y in range(planes):
                chip = ((z + shift) % ring) * PAIR + (x ^ flip)
                if chip // per_plane == (y - turn) % planes:
                    pairs.append((device(z, x, c) * planes + y, device(z + shift, x ^ flip, c) * planes + y))
        return pairs

    def route_back(shift, flip):
        turn = cross(shift, flip)
        return [(b, a - a % planes + (a - turn) % planes) for a, b in route(shift, flip)]

    def cross(shift, flip):
        return 1 if shift and flip else 0

    both = ("row", "col")
    permute = lax.ppermute

    keeping = keep_mask.astype(jnp.float32)
    change, rest = prepare(dense_weight, start_iterate, start_multiplier, keep_mask, per_plane)
    sibling = permute(hessian, "row", to_sibling)

    def piece(shift, flip):
        turn = cross(shift, flip)
        chip = ((place + shift) % ring) * PAIR + (pair ^ flip)
        first_chip = ((plane - turn) % planes) * per_plane
        source = rest_by[turn]
        part = lax.dynamic_index_in_dim(source, jnp.clip(chip - first_chip, 0, per_plane - 1), 0, keepdims=False)
        part = part.reshape(half, CORES, depth)
        part = jnp.where(core == 0, part, part[:, ::-1]).transpose(1, 0, 2)
        if shift == 0 and flip == 0:
            return jnp.where(chip // per_plane == plane, part, 0.0)
        return permute(part, both, route(shift, flip))

    def sum_planes(part):
        others = [permute(part, "col", [(y, (y + turn) % planes) for y in range(planes)]) for turn in range(1, planes)]
        return functools.reduce(jnp.add, others) if others else jnp.zeros_like(part)

    rest_by = {0: rest}
    near, far, added = {0: change}, {}, {}
    product, mine, other, changed, kept, sent, swapped, back = {}, {}, {}, {}, {}, {}, {}, {}
    total = None
    start = max(ring, 4)
    returns = [(0, 0, 5), (0, 1, 4)] + [(g, flip, g + 2 + (g == 1 and flip)) for g in range(1, ring) for flip in range(PAIR)]
    for window in range(start + ring):
        fresh = []

        def put(where, key, value):
            where[key] = value
            fresh.append((where, key))

        if window < ring - 1:
            put(near, window + 1, permute(near[window], "row", to_next))
        if window < ring:
            put(far, window, permute(near[window], "row", to_pair))
        if window == 0:
            put(rest_by, 1, permute(rest, "col", [(y, (y + 1) % planes) for y in range(planes)]))
        elif window < ring:
            for flip in range(PAIR):
                added[window, flip] = piece(window, flip)
        if window == 1:
            for flip in range(PAIR):
                put(added, (0, flip), piece(0, flip))
        closing = window - start + 1
        if closing >= 1:
            if total is not None:
                total = permute(total, "row", to_next)
            put(swapped, closing % ring, permute(sent[closing % ring], "row", to_pair))
        group = window - 2
        if 1 <= group < ring:
            put(changed, group, mine[group] + other[group])
        if group == 1:
            put(changed, 0, mine[0] + other[0])
        group = window - 1
        if 0 <= group < ring:
            put(product, group, first(near[group], far[group], hessian, sibling))
        for group in (0, 1) if window == 2 else (window - 1,) if 2 < window <= ring else ():
            put(mine, group, product[group] + jnp.concatenate([added[group, 0], added[group, 1]], axis=1))
            put(other, group, sum_planes(mine[group]))
        group = window - 2
        if window == start + ring - 2:
            group = 0
        if (1 <= group < ring) or window == start + ring - 2:
            keep, send = second(changed[group], hessian, sibling)
            put(kept, group, keep)
            put(sent, group, send)
        for group, flip, when in returns:
            if when == window:
                part = changed[group][:, flip * half : (flip + 1) * half]
                if group or flip:
                    part = permute(part, both, route_back(group, flip))
                put(back, (group, flip), part)
        values = [where[key] for where, key in fresh]
        values, sibling, total, rest_by[0] = lax.optimization_barrier((values, sibling, total, rest_by[0]))
        for (where, key), value in zip(fresh, values):
            where[key] = value
        if closing >= 1:
            part = kept[closing % ring] + swapped[closing % ring]
            total = part if total is None else total + part

    back = jnp.stack([back[shift, flip] for shift in range(ring) for flip in range(PAIR)])
    blocks = []
    for block in range(per_plane):
        chip = plane * per_plane + block
        slot = ((chip // PAIR - place) % ring) * PAIR + ((chip % PAIR) ^ pair)
        blocks.append(lax.dynamic_index_in_dim(back, slot, 0, keepdims=False))
    blocks = jnp.stack(blocks)
    blocks = jnp.where(core == 0, blocks, blocks[:, ::-1])
    iterate = blocks.transpose(0, 1, 3, 2).reshape(columns, half) + dense_weight

    projected = keeping * (iterate + start_multiplier)
    multiplier = start_multiplier + iterate - projected
    iterate = iterate - step_size * (total.T + penalty * (iterate - projected + multiplier))
    projected = keeping * (iterate + multiplier)
    multiplier = multiplier + iterate - projected
    return (iterate, projected, multiplier)


def solution(mesh):
    return jax.shard_map(
        functools.partial(per_device, mesh.shape["row"], mesh.shape["col"]),
        mesh=mesh,
        in_specs=(
            P("row", "col"),
            P("col", "row"),
            P("col", "row"),
            P("col", "row"),
            P("col", "row"),
        ),
        out_specs=(P("col", "row"), P("col", "row"), P("col", "row")),
        check_vma=False,
    )
```

```python
import functools

import jax
import jax.numpy as jnp
from jax import lax
from jax.experimental import pallas as pl
from jax.experimental.pallas import tpu as pltpu
from jax.sharding import PartitionSpec as P

step_size = 0.25
penalty = 1.0

CORES = 2
PAIR = 2
VMEM_BYTES = 48 * 1024 * 1024


def split(value):
    high = value.astype(jnp.bfloat16)
    low = (value - high.astype(jnp.float32)).astype(jnp.bfloat16)
    return high, low


def dot_f32(left, right, rows, dims):
    high, low = split(right)
    both = lax.dot_general(left[...], high, dims, preferred_element_type=jnp.float32)
    cross = lax.dot_general(left[:rows], low, dims, preferred_element_type=jnp.float32)
    return both[:rows] + (both[rows:] + cross)


def first_kernel(near_ref, far_ref, own_ref, sib_ref, out_ref, parts):
    half = near_ref.shape[0]
    rows = 2 * half

    @pl.when(pl.program_id(0) == 0)
    def _():
        parts[:half], parts[rows : rows + half] = split(near_ref[...])
        parts[half:rows], parts[rows + half :] = split(far_ref[...])

    tile = own_ref.shape[0]
    rows_of_h = jnp.concatenate([own_ref[...], sib_ref[...]], axis=0)
    product = dot_f32(parts, rows_of_h, rows, (((1,), (1,)), ((), ())))
    for which in range(2):
        out_ref[which] = -step_size * product[:, which * tile : (which + 1) * tile]


def first(near, far, own, sib):
    half, depth = near.shape
    rows = own.shape[0]
    tile = 128 if rows % 128 == 0 else rows
    whole = pl.BlockSpec((half, depth), lambda i: (0, 0))
    band = pl.BlockSpec((tile, depth), lambda i: (i, 0))
    return pl.pallas_call(
        first_kernel,
        grid=(rows // tile,),
        in_specs=[whole, whole, band, band],
        out_specs=pl.BlockSpec((2, 2 * half, tile), lambda i: (0, 0, i)),
        out_shape=jax.ShapeDtypeStruct((2, 2 * half, rows), jnp.float32),
        scratch_shapes=[pltpu.VMEM((4 * half, depth), jnp.bfloat16)],
        compiler_params=pltpu.CompilerParams(vmem_limit_bytes=VMEM_BYTES),
        cost_estimate=pl.CostEstimate(
            flops=rows * depth, bytes_accessed=rows * depth, transcendentals=0
        ),
        name="first_product",
    )(near, far, own, sib)


def second_kernel(change_ref, own_ref, sib_ref, near_ref, far_ref, parts):
    _, rows, depth = change_ref.shape
    half = rows // 2

    @pl.when(pl.program_id(0) == 0)
    def _():
        for which in range(2):
            places = slice(which * depth, (which + 1) * depth)
            parts[:rows, places], parts[rows:, places] = split(change_ref[which])

    rows_of_h = jnp.concatenate([own_ref[...], sib_ref[...]], axis=0)
    product = dot_f32(parts, rows_of_h, rows, (((1,), (0,)), ((), ())))
    near_ref[...] = product[:half]
    far_ref[...] = product[half:]


def second(change, own, sib):
    _, rows, depth = change.shape
    half = rows // 2
    columns = own.shape[1]
    tile = next((t for t in (512, 256, 128) if columns % t == 0), columns)
    band = pl.BlockSpec((depth, tile), lambda i: (0, i))
    out = pl.BlockSpec((half, tile), lambda i: (0, i))
    return pl.pallas_call(
        second_kernel,
        grid=(columns // tile,),
        in_specs=[pl.BlockSpec((2, rows, depth), lambda i: (0, 0, 0)), band, band],
        out_specs=[out, out],
        out_shape=[jax.ShapeDtypeStruct((half, columns), jnp.float32)] * 2,
        scratch_shapes=[pltpu.VMEM((2 * rows, 2 * depth), jnp.bfloat16)],
        compiler_params=pltpu.CompilerParams(vmem_limit_bytes=VMEM_BYTES),
        cost_estimate=pl.CostEstimate(
            flops=depth * columns, bytes_accessed=depth * columns, transcendentals=0
        ),
        name="second_product",
    )(change, own, sib)


def per_device(rows_of, planes, hessian, dense_weight, start_iterate, start_multiplier, keep_mask):
    ring = rows_of // (CORES * PAIR)
    chips = ring * PAIR
    per_plane = chips // planes
    depth, columns = hessian.shape
    half = dense_weight.shape[1]
    row = lax.axis_index("row")
    plane = lax.axis_index("col")
    core = row % CORES
    pair = (row // CORES) % PAIR
    place = row // (CORES * PAIR)

    def device(z, x, c):
        return ((z % ring) * PAIR + x) * CORES + c

    everyone = [(z, x, c) for z in range(ring) for x in range(PAIR) for c in range(CORES)]
    to_sibling = [(device(z, x, c), device(z, x, 1 - c)) for z, x, c in everyone]
    to_pair = [(device(z, x, c), device(z, x ^ 1, c)) for z, x, c in everyone]
    to_next = [(device(z, x, c), device(z + 1, x, c)) for z, x, c in everyone]

    def route(shift, flip):
        turn = cross(shift, flip)
        pairs = []
        for z, x, c in everyone:
            for y in range(planes):
                chip = ((z + shift) % ring) * PAIR + (x ^ flip)
                if chip // per_plane == (y - turn) % planes:
                    pairs.append((device(z, x, c) * planes + y, device(z + shift, x ^ flip, c) * planes + y))
        return pairs

    def route_back(shift, flip):
        turn = cross(shift, flip)
        return [(b, a - a % planes + (a - turn) % planes) for a, b in route(shift, flip)]

    def cross(shift, flip):
        return 1 if shift and flip else 0

    both = ("row", "col")
    permute = lax.ppermute

    dense, begun, dual = dense_weight.T, start_iterate.T, start_multiplier.T
    keeping = keep_mask.T.astype(jnp.float32)
    change = begun - dense
    sibling = permute(hessian, "row", to_sibling)
    rest = begun - step_size * (penalty * (begun - keeping * (begun + dual) + dual)) - dense
    rest_by = [rest, permute(rest, "col", [(y, (y + 1) % planes) for y in range(planes)])]

    def piece(shift, flip):
        turn = cross(shift, flip)
        chip = ((place + shift) % ring) * PAIR + (pair ^ flip)
        at = jnp.clip(chip - ((plane - turn) % planes) * per_plane, 0, per_plane - 1)
        part = lax.dynamic_slice_in_dim(rest_by[turn], at * CORES * depth, CORES * depth, 1)
        part = part.reshape(half, CORES, depth)
        part = jnp.where(core == 0, part, part[:, ::-1]).transpose(1, 0, 2)
        if shift == 0 and flip == 0:
            return jnp.where(chip // per_plane == plane, part, 0.0)
        return permute(part, both, route(shift, flip))

    def sum_planes(part):
        others = [permute(part, "col", [(y, (y + turn) % planes) for y in range(planes)]) for turn in range(1, planes)]
        return functools.reduce(jnp.add, others) if others else jnp.zeros_like(part)

    near = {0: change, 1: permute(change, "row", to_next)}
    far = {0: permute(change, "row", to_pair)}
    rest_by = dict(enumerate(rest_by))
    added, mine, other, changed, kept, sums, swapped, back = {}, {}, {}, {}, {}, {}, {}, {}
    last = (near, 0)

    def meet(*entries):
        entries = list(dict.fromkeys([(id(where), key) for where, key in entries + (last,)]))
        wheres = {id(where): where for where in (near, far, rest_by, added, mine, other, changed, kept, sums, swapped, back)}
        values = lax.optimization_barrier([wheres[which][key] for which, key in entries])
        for (which, key), value in zip(entries, values):
            wheres[which][key] = value

    def flips(where, group):
        return [(where, (group, flip)) for flip in range(PAIR)]

    def add_pieces(group):
        if group < ring:
            meet(*((rest_by, turn) for turn in rest_by))
            for flip in range(PAIR):
                added[group, flip] = piece(group, flip)

    def send_back(group):
        meet((changed, group))
        for flip in range(PAIR):
            rows = changed[group][:, flip * half : (flip + 1) * half]
            back[group, flip] = permute(rows, both, route_back(group, flip)) if group or flip else rows

    def run_first(group):
        nonlocal last
        after = group + 1
        if after < ring:
            meet((far, group), (near, after))
            far[after] = permute(near[after], "row", to_pair)
            if after + 1 < ring:
                near[after + 1] = permute(near[after], "row", to_next)
        if group == 0:
            add_pieces(1)
        meet((far, group), (near, group))
        mine[group] = first(near[group], far[group], hessian, sibling)
        last = (mine, group)

    def run_join(group):
        meet(*flips(added, group))
        mine[group] = mine[group] + jnp.concatenate([added[group, flip] for flip in range(PAIR)], axis=1)
        other[group] = sum_planes(mine[group])
        if group:
            add_pieces(group + 1)

    def run_change(group):
        nonlocal last
        meet((other, group), (mine, group))
        changed[group] = mine[group] + other[group]
        last = (changed, group)

    def run_second(group):
        nonlocal last
        meet((changed, group))
        kept[group], sent = second(changed[group], hessian, sibling)
        swapped[group] = permute(sent, "row", to_pair)
        last = (kept, group)

    def run_add(group, total, *following):
        meet((swapped, group), (kept, group))
        part = kept[group] + swapped[group]
        sums[group] = part if total is None else total + part
        if following:
            meet((sums, group), following)
        return permute(sums[group], "row", to_next)

    added[0, 1] = piece(0, 1)
    added[0, 0] = piece(0, 0)
    total = None
    for group in range(ring):
        run_first(group)
        if group >= 3:
            meet(*flips(back, group - 2))
        run_join(group)
        if group >= 3:
            send_back(group - 1)
        if group == 1:
            run_change(0)
        if group == 2:
            run_change(1)
        if group >= 2:
            run_second(group - 1)
            run_change(group)
            if group == 2:
                send_back(1)
        if group >= 3:
            total = run_add(group - 2, total, *((changed, group) if group == ring - 1 else (near, group + 1)))
    meet(*flips(back, ring - 2))
    send_back(ring - 1)
    run_second(ring - 1)
    meet(*flips(back, ring - 1))
    total = run_add(ring - 2, total, changed, 0)
    run_second(0)
    send_back(0)
    total = run_add(ring - 1, total)
    gradient = total + (kept[0] + swapped[0])

    back = jnp.stack([back[shift, flip] for shift in range(ring) for flip in range(PAIR)])
    blocks = []
    for block in range(per_plane):
        chip = plane * per_plane + block
        slot = ((chip // PAIR - place) % ring) * PAIR + ((chip % PAIR) ^ pair)
        part = lax.dynamic_index_in_dim(back, slot, 0, keepdims=False)
        part = jnp.where(core == 0, part, part[::-1])
        blocks += [part[0], part[1]]
    iterate = jnp.concatenate(blocks, axis=1) + dense

    projected = keeping * (iterate + dual)
    multiplier = dual + iterate - projected
    iterate = iterate - step_size * (gradient + penalty * (iterate - projected + multiplier))
    projected = keeping * (iterate + multiplier)
    multiplier = multiplier + iterate - projected
    return (iterate.T, projected.T, multiplier.T)


def solution(mesh):
    return jax.shard_map(
        functools.partial(per_device, mesh.shape["row"], mesh.shape["col"]),
        mesh=mesh,
        in_specs=(
            P("row", "col"),
            P("col", "row"),
            P("col", "row"),
            P("col", "row"),
            P("col", "row"),
        ),
        out_specs=(P("col", "row"), P("col", "row"), P("col", "row")),
        check_vma=False,
    )
```

```python
import functools

import jax
import jax.numpy as jnp
from jax import lax
from jax.experimental import pallas as pl
from jax.experimental.pallas import tpu as pltpu
from jax.sharding import PartitionSpec as P

step_size = 0.25
penalty = 1.0

CORES = 2
PAIR = 2
VMEM_BYTES = 48 * 1024 * 1024


def split(value):
    high = value.astype(jnp.bfloat16)
    low = (value - high.astype(jnp.float32)).astype(jnp.bfloat16)
    return high, low


def dot_f32(left, right, rows, dims):
    high, low = split(right)
    both = lax.dot_general(left[...], high, dims, preferred_element_type=jnp.float32)
    cross = lax.dot_general(left[:rows], low, dims, preferred_element_type=jnp.float32)
    return both[:rows] + (both[rows:] + cross)


def first_kernel(near_ref, far_ref, own_ref, sib_ref, out_ref, parts):
    half = near_ref.shape[0]
    rows = 2 * half

    @pl.when(pl.program_id(0) == 0)
    def _():
        parts[:half], parts[rows : rows + half] = split(near_ref[...])
        parts[half:rows], parts[rows + half :] = split(far_ref[...])

    tile = own_ref.shape[0]
    rows_of_h = jnp.concatenate([own_ref[...], sib_ref[...]], axis=0)
    product = dot_f32(parts, rows_of_h, rows, (((1,), (1,)), ((), ())))
    for which in range(2):
        out_ref[which] = -step_size * product[:, which * tile : (which + 1) * tile]


def first(near, far, own, sib):
    half, depth = near.shape
    rows = own.shape[0]
    tile = 128 if rows % 128 == 0 else rows
    whole = pl.BlockSpec((half, depth), lambda i: (0, 0))
    band = pl.BlockSpec((tile, depth), lambda i: (i, 0))
    return pl.pallas_call(
        first_kernel,
        grid=(rows // tile,),
        in_specs=[whole, whole, band, band],
        out_specs=pl.BlockSpec((2, 2 * half, tile), lambda i: (0, 0, i)),
        out_shape=jax.ShapeDtypeStruct((2, 2 * half, rows), jnp.float32),
        scratch_shapes=[pltpu.VMEM((4 * half, depth), jnp.bfloat16)],
        compiler_params=pltpu.CompilerParams(vmem_limit_bytes=VMEM_BYTES),
        cost_estimate=pl.CostEstimate(
            flops=3 * 2 * 4 * half * depth * rows, bytes_accessed=8 * rows * depth, transcendentals=0
        ),
        name="first_product",
    )(near, far, own, sib)


def second_kernel(change_ref, own_ref, sib_ref, near_ref, far_ref, parts):
    _, rows, depth = change_ref.shape
    half = rows // 2

    @pl.when(pl.program_id(0) == 0)
    def _():
        for which in range(2):
            places = slice(which * depth, (which + 1) * depth)
            parts[:rows, places], parts[rows:, places] = split(change_ref[which])

    rows_of_h = jnp.concatenate([own_ref[...], sib_ref[...]], axis=0)
    product = dot_f32(parts, rows_of_h, rows, (((1,), (0,)), ((), ())))
    near_ref[...] = product[:half]
    far_ref[...] = product[half:]


def second(change, own, sib):
    _, rows, depth = change.shape
    half = rows // 2
    columns = own.shape[1]
    tile = next((t for t in (512, 256, 128) if columns % t == 0), columns)
    band = pl.BlockSpec((depth, tile), lambda i: (0, i))
    out = pl.BlockSpec((half, tile), lambda i: (0, i))
    return pl.pallas_call(
        second_kernel,
        grid=(columns // tile,),
        in_specs=[pl.BlockSpec((2, rows, depth), lambda i: (0, 0, 0)), band, band],
        out_specs=[out, out],
        out_shape=[jax.ShapeDtypeStruct((half, columns), jnp.float32)] * 2,
        scratch_shapes=[pltpu.VMEM((2 * rows, 2 * depth), jnp.bfloat16)],
        compiler_params=pltpu.CompilerParams(vmem_limit_bytes=VMEM_BYTES),
        cost_estimate=pl.CostEstimate(
            flops=3 * 2 * 2 * rows * depth * columns, bytes_accessed=8 * depth * columns, transcendentals=0
        ),
        name="second_product",
    )(change, own, sib)


def per_device(rows_of, planes, hessian, dense_weight, start_iterate, start_multiplier, keep_mask):
    ring = rows_of // (CORES * PAIR)
    chips = ring * PAIR
    per_plane = chips // planes
    depth, columns = hessian.shape
    half = dense_weight.shape[1]
    row = lax.axis_index("row")
    plane = lax.axis_index("col")
    core = row % CORES
    pair = (row // CORES) % PAIR
    place = row // (CORES * PAIR)

    def device(z, x, c):
        return ((z % ring) * PAIR + x) * CORES + c

    everyone = [(z, x, c) for z in range(ring) for x in range(PAIR) for c in range(CORES)]
    to_sibling = [(device(z, x, c), device(z, x, 1 - c)) for z, x, c in everyone]
    to_pair = [(device(z, x, c), device(z, x ^ 1, c)) for z, x, c in everyone]
    to_next = [(device(z, x, c), device(z + 1, x, c)) for z, x, c in everyone]

    def route(shift, flip):
        turn = cross(shift, flip)
        pairs = []
        for z, x, c in everyone:
            for y in range(planes):
                chip = ((z + shift) % ring) * PAIR + (x ^ flip)
                if chip // per_plane == (y - turn) % planes:
                    pairs.append((device(z, x, c) * planes + y, device(z + shift, x ^ flip, c) * planes + y))
        return pairs

    def route_back(shift, flip):
        turn = cross(shift, flip)
        return [(b, a - a % planes + (a - turn) % planes) for a, b in route(shift, flip)]

    def cross(shift, flip):
        return 1 if shift and flip else 0

    both = ("row", "col")
    permute = lax.ppermute

    dense, begun, dual = dense_weight.T, start_iterate.T, start_multiplier.T
    keeping = keep_mask.T.astype(jnp.float32)
    change = begun - dense
    sibling = permute(hessian, "row", to_sibling)
    rest = begun - step_size * (penalty * (begun - keeping * (begun + dual) + dual)) - dense
    def piece(shift, flip):
        turn = cross(shift, flip)
        chip = ((place + shift) % ring) * PAIR + (pair ^ flip)
        at = jnp.clip(chip - ((plane - turn) % planes) * per_plane, 0, per_plane - 1)
        part = lax.dynamic_slice_in_dim(rest_by[turn], at * CORES * depth, CORES * depth, 1)
        part = part.reshape(half, CORES, depth)
        part = jnp.where(core == 0, part, part[:, ::-1]).transpose(1, 0, 2)
        if shift == 0 and flip == 0:
            return jnp.where(chip // per_plane == plane, part, 0.0)
        return permute(part, both, route(shift, flip))

    def sum_planes(part):
        others = [permute(part, "col", [(y, (y + turn) % planes) for y in range(planes)]) for turn in range(1, planes)]
        return functools.reduce(jnp.add, others) if others else jnp.zeros_like(part)

    rest_by = {0: rest}
    near, far, added = {0: change}, {}, {}
    product, mine, other, changed, kept, sent, swapped, back = {}, {}, {}, {}, {}, {}, {}, {}
    total = None
    start = max(ring, 4)
    returns = {group + 2: [(group, 0), (group, 1)] for group in range(2, ring - 1)}
    returns.setdefault(3, []).append((1, 0))
    returns.setdefault(start + 1, []).extend([(1, 1), (ring - 1, 0)])
    returns.setdefault(start + 2, []).extend([(ring - 1, 1), (0, 0), (0, 1)])
    for window in range(start + ring):
        fresh = []

        def put(where, key, value):
            where[key] = value
            fresh.append((where, key))

        if window < ring - 1:
            put(near, window + 1, permute(near[window], "row", to_next))
        if window < ring:
            put(far, window, permute(near[window], "row", to_pair))
        if window == 0:
            put(rest_by, 1, permute(rest, "col", [(y, (y + 1) % planes) for y in range(planes)]))
        elif window < ring:
            for flip in range(PAIR):
                added[window, flip] = piece(window, flip)
                if window == ring - 1:
                    fresh.append((added, (window, flip)))
        closing = window - start + 1
        if closing >= 1:
            if total is not None:
                total = permute(total, "row", to_next)
            put(swapped, closing % ring, permute(sent[closing % ring], "row", to_pair))
        group = window - 2
        if 1 <= group < ring:
            put(changed, group, mine[group] + other[group])
        if window == start:
            for flip in range(PAIR):
                put(added, (0, flip), piece(0, flip))
        if window == start + 1:
            put(mine, 0, product[0] + jnp.concatenate([added[0, 0], added[0, 1]], axis=1))
            put(other, 0, sum_planes(mine[0]))
        if window == start + 2:
            put(changed, 0, mine[0] + other[0])
        group = window - 1
        if 0 <= group < ring:
            put(product, group, first(near[group], far[group], hessian, sibling))
            if group:
                put(mine, group, product[group] + jnp.concatenate([added[group, 0], added[group, 1]], axis=1))
                put(other, group, sum_planes(mine[group]))
        group = 0 if window == start + ring - 2 else window - 2
        if 1 <= group < ring or window == start + ring - 2:
            keep, send = second(changed[group], hessian, sibling)
            put(kept, group, keep)
            put(sent, group, send)
        for group, flip in returns.get(window, []):
            rows = changed[group][:, flip * half : (flip + 1) * half]
            put(back, (group, flip), permute(rows, both, route_back(group, flip)) if group or flip else rows)
        values = [where[key] for where, key in fresh]
        values, sibling, total, rest_by[0] = lax.optimization_barrier((values, sibling, total, rest_by[0]))
        for (where, key), value in zip(fresh, values):
            where[key] = value
        if closing >= 1:
            part = kept[closing % ring] + swapped[closing % ring]
            total = part if total is None else total + part
    gradient = total

    back = jnp.stack([back[shift, flip] for shift in range(ring) for flip in range(PAIR)])
    blocks = []
    for block in range(per_plane):
        chip = plane * per_plane + block
        slot = ((chip // PAIR - place) % ring) * PAIR + ((chip % PAIR) ^ pair)
        part = lax.dynamic_index_in_dim(back, slot, 0, keepdims=False)
        part = jnp.where(core == 0, part, part[::-1])
        blocks += [part[0], part[1]]
    iterate = jnp.concatenate(blocks, axis=1) + dense

    projected = keeping * (iterate + dual)
    multiplier = dual + iterate - projected
    iterate = iterate - step_size * (gradient + penalty * (iterate - projected + multiplier))
    projected = keeping * (iterate + multiplier)
    multiplier = multiplier + iterate - projected
    return (iterate.T, projected.T, multiplier.T)


def solution(mesh):
    return jax.shard_map(
        functools.partial(per_device, mesh.shape["row"], mesh.shape["col"]),
        mesh=mesh,
        in_specs=(
            P("row", "col"),
            P("col", "row"),
            P("col", "row"),
            P("col", "row"),
            P("col", "row"),
        ),
        out_specs=(P("col", "row"), P("col", "row"), P("col", "row")),
        check_vma=False,
    )
```

```python
import functools

import jax
import jax.numpy as jnp
from jax import lax
from jax.experimental import pallas as pl
from jax.experimental.pallas import tpu as pltpu
from jax.sharding import PartitionSpec as P

step_size = 0.25
penalty = 1.0

CORES = 2
PAIR = 2
VMEM_BYTES = 48 * 1024 * 1024


def split(value):
    high = value.astype(jnp.bfloat16)
    low = (value - high.astype(jnp.float32)).astype(jnp.bfloat16)
    return high, low


def dot_f32(left, right, rows, dims):
    high, low = split(right)
    both = lax.dot_general(left[...], high, dims, preferred_element_type=jnp.float32)
    cross = lax.dot_general(left[:rows], low, dims, preferred_element_type=jnp.float32)
    return both[:rows] + (both[rows:] + cross)


def first_kernel(near_ref, far_ref, own_ref, sib_ref, out_ref, parts):
    half = near_ref.shape[0]
    rows = 2 * half

    @pl.when(pl.program_id(0) == 0)
    def _():
        parts[:half], parts[rows : rows + half] = split(near_ref[...])
        parts[half:rows], parts[rows + half :] = split(far_ref[...])

    tile = own_ref.shape[0]
    rows_of_h = jnp.concatenate([own_ref[...], sib_ref[...]], axis=0)
    product = dot_f32(parts, rows_of_h, rows, (((1,), (1,)), ((), ())))
    for which in range(2):
        out_ref[which] = -step_size * product[:, which * tile : (which + 1) * tile]


def first(near, far, own, sib):
    half, depth = near.shape
    rows = own.shape[0]
    tile = 128 if rows % 128 == 0 else rows
    whole = pl.BlockSpec((half, depth), lambda i: (0, 0))
    band = pl.BlockSpec((tile, depth), lambda i: (i, 0))
    return pl.pallas_call(
        first_kernel,
        grid=(rows // tile,),
        in_specs=[whole, whole, band, band],
        out_specs=pl.BlockSpec((2, 2 * half, tile), lambda i: (0, 0, i)),
        out_shape=jax.ShapeDtypeStruct((2, 2 * half, rows), jnp.float32),
        scratch_shapes=[pltpu.VMEM((4 * half, depth), jnp.bfloat16)],
        compiler_params=pltpu.CompilerParams(vmem_limit_bytes=VMEM_BYTES),
        cost_estimate=pl.CostEstimate(
            flops=3 * 2 * 4 * half * depth * rows, bytes_accessed=8 * rows * depth, transcendentals=0
        ),
        name="first_product",
    )(near, far, own, sib)


def second_kernel(change_ref, own_ref, sib_ref, near_ref, far_ref, parts):
    _, rows, depth = change_ref.shape
    half = rows // 2

    @pl.when(pl.program_id(0) == 0)
    def _():
        for which in range(2):
            places = slice(which * depth, (which + 1) * depth)
            parts[:rows, places], parts[rows:, places] = split(change_ref[which])

    rows_of_h = jnp.concatenate([own_ref[...], sib_ref[...]], axis=0)
    product = dot_f32(parts, rows_of_h, rows, (((1,), (0,)), ((), ())))
    near_ref[...] = product[:half]
    far_ref[...] = product[half:]


def second(change, own, sib):
    _, rows, depth = change.shape
    half = rows // 2
    columns = own.shape[1]
    tile = next((t for t in (512, 256, 128) if columns % t == 0), columns)
    band = pl.BlockSpec((depth, tile), lambda i: (0, i))
    out = pl.BlockSpec((half, tile), lambda i: (0, i))
    return pl.pallas_call(
        second_kernel,
        grid=(columns // tile,),
        in_specs=[pl.BlockSpec((2, rows, depth), lambda i: (0, 0, 0)), band, band],
        out_specs=[out, out],
        out_shape=[jax.ShapeDtypeStruct((half, columns), jnp.float32)] * 2,
        scratch_shapes=[pltpu.VMEM((2 * rows, 2 * depth), jnp.bfloat16)],
        compiler_params=pltpu.CompilerParams(vmem_limit_bytes=VMEM_BYTES),
        cost_estimate=pl.CostEstimate(
            flops=3 * 2 * 2 * rows * depth * columns, bytes_accessed=8 * depth * columns, transcendentals=0
        ),
        name="second_product",
    )(change, own, sib)


def per_device(rows_of, planes, hessian, dense_weight, start_iterate, start_multiplier, keep_mask):
    ring = rows_of // (CORES * PAIR)
    chips = ring * PAIR
    per_plane = chips // planes
    depth, columns = hessian.shape
    half = dense_weight.shape[1]
    row = lax.axis_index("row")
    plane = lax.axis_index("col")
    core = row % CORES
    pair = (row // CORES) % PAIR
    place = row // (CORES * PAIR)

    def device(z, x, c):
        return ((z % ring) * PAIR + x) * CORES + c

    everyone = [(z, x, c) for z in range(ring) for x in range(PAIR) for c in range(CORES)]
    to_sibling = [(device(z, x, c), device(z, x, 1 - c)) for z, x, c in everyone]
    to_pair = [(device(z, x, c), device(z, x ^ 1, c)) for z, x, c in everyone]
    to_next = [(device(z, x, c), device(z + 1, x, c)) for z, x, c in everyone]

    def route(shift, flip):
        turn = cross(shift, flip)
        pairs = []
        for z, x, c in everyone:
            for y in range(planes):
                chip = ((z + shift) % ring) * PAIR + (x ^ flip)
                if chip // per_plane == (y - turn) % planes:
                    pairs.append((device(z, x, c) * planes + y, device(z + shift, x ^ flip, c) * planes + y))
        return pairs

    def route_back(shift, flip):
        turn = cross(shift, flip)
        return [(b, a - a % planes + (a - turn) % planes) for a, b in route(shift, flip)]

    def cross(shift, flip):
        return 1 if shift and flip else 0

    both = ("row", "col")
    permute = lax.ppermute

    dense, begun, dual = dense_weight.T, start_iterate.T, start_multiplier.T
    keeping = keep_mask.T.astype(jnp.float32)
    change = begun - dense
    sibling = permute(hessian, "row", to_sibling)
    rest = begun - step_size * (penalty * (begun - keeping * (begun + dual) + dual)) - dense
    def piece(shift, flip):
        turn = cross(shift, flip)
        chip = ((place + shift) % ring) * PAIR + (pair ^ flip)
        at = jnp.clip(chip - ((plane - turn) % planes) * per_plane, 0, per_plane - 1)
        part = lax.dynamic_slice_in_dim(rest_by[turn], at * CORES * depth, CORES * depth, 1)
        part = part.reshape(half, CORES, depth)
        part = jnp.where(core == 0, part, part[:, ::-1]).transpose(1, 0, 2)
        if shift == 0 and flip == 0:
            return jnp.where(chip // per_plane == plane, part, 0.0)
        return permute(part, both, route(shift, flip))

    def sum_planes(part):
        others = [permute(part, "col", [(y, (y + turn) % planes) for y in range(planes)]) for turn in range(1, planes)]
        return functools.reduce(jnp.add, others) if others else jnp.zeros_like(part)

    rest_by = {0: rest}
    near, far, added = {0: change}, {}, {}
    product, mine, other, changed, kept, sent, swapped, back = {}, {}, {}, {}, {}, {}, {}, {}
    total = None
    start = max(ring, 4)
    returns = {group + 2: [(group, 0), (group, 1)] for group in range(2, ring)}
    returns.setdefault(3, []).append((1, 0))
    returns.setdefault(4, []).append((1, 1))
    returns.setdefault(start + 2, []).extend([(0, 0), (0, 1)])
    for window in range(start + ring):
        fresh = []

        def put(where, key, value):
            where[key] = value
            fresh.append((where, key))

        if window < ring - 1:
            put(near, window + 1, permute(near[window], "row", to_next))
        if window < ring:
            put(far, window, permute(near[window], "row", to_pair))
        if window == 0:
            rest_by[1] = (permute(rest, "col", [(y, (y + 1) % planes) for y in range(planes)]))
        elif window < ring:
            for flip in range(PAIR):
                added[window, flip] = piece(window, flip)
                if window == ring - 1:
                    fresh.append((added, (window, flip)))
                if window == 1:
                    added[0, flip] = piece(0, flip)
        closing = window - start + 1
        if closing >= 1:
            if total is not None:
                total = permute(total, "row", to_next)
            put(swapped, closing % ring, permute(sent[closing % ring], "row", to_pair))
        group = window - 2
        if 1 <= group < ring:
            put(changed, group, mine[group] + other[group])
        if window == 2:
            fresh += [(added, (0, flip)) for flip in range(PAIR)]
        if window == start + 1:
            put(mine, 0, product[0] + jnp.concatenate([added[0, 0], added[0, 1]], axis=1))
            put(other, 0, sum_planes(mine[0]))
        if window == start + 2:
            put(changed, 0, mine[0] + other[0])
        group = window - 1
        if 0 <= group < ring:
            put(product, group, first(near[group], far[group], hessian, sibling))
            if group:
                put(mine, group, product[group] + jnp.concatenate([added[group, 0], added[group, 1]], axis=1))
                put(other, group, sum_planes(mine[group]))
        group = 0 if window == start + ring - 2 else window - 2
        if 1 <= group < ring or window == start + ring - 2:
            keep, send = second(changed[group], hessian, sibling)
            put(kept, group, keep)
            put(sent, group, send)
        for group, flip in returns.get(window, []):
            rows = changed[group][:, flip * half : (flip + 1) * half]
            put(back, (group, flip), permute(rows, both, route_back(group, flip)) if group or flip else rows)
        values = [where[key] for where, key in fresh]
        values, sibling, total, rest_by = lax.optimization_barrier((values, sibling, total, rest_by))
        for (where, key), value in zip(fresh, values):
            where[key] = value
        if closing >= 1:
            part = kept[closing % ring] + swapped[closing % ring]
            total = part if total is None else total + part
    gradient = total

    back = jnp.stack([back[shift, flip] for shift in range(ring) for flip in range(PAIR)])
    blocks = []
    for block in range(per_plane):
        chip = plane * per_plane + block
        slot = ((chip // PAIR - place) % ring) * PAIR + ((chip % PAIR) ^ pair)
        part = lax.dynamic_index_in_dim(back, slot, 0, keepdims=False)
        part = jnp.where(core == 0, part, part[::-1])
        blocks += [part[0], part[1]]
    iterate = jnp.concatenate(blocks, axis=1) + dense

    projected = keeping * (iterate + dual)
    multiplier = dual + iterate - projected
    iterate = iterate - step_size * (gradient + penalty * (iterate - projected + multiplier))
    projected = keeping * (iterate + multiplier)
    multiplier = multiplier + iterate - projected
    return (iterate.T, projected.T, multiplier.T)


def solution(mesh):
    return jax.shard_map(
        functools.partial(per_device, mesh.shape["row"], mesh.shape["col"]),
        mesh=mesh,
        in_specs=(
            P("row", "col"),
            P("col", "row"),
            P("col", "row"),
            P("col", "row"),
            P("col", "row"),
        ),
        out_specs=(P("col", "row"), P("col", "row"), P("col", "row")),
        check_vma=False,
    )
```

```python
import functools

import jax
import jax.numpy as jnp
from jax import lax
from jax.experimental import pallas as pl
from jax.experimental.pallas import tpu as pltpu
from jax.sharding import PartitionSpec as P

step_size = 0.25
penalty = 1.0

CORES = 2
PAIR = 2
VMEM_BYTES = 48 * 1024 * 1024


def split(value):
    high = value.astype(jnp.bfloat16)
    low = (value - high.astype(jnp.float32)).astype(jnp.bfloat16)
    return high, low


def dot_f32(left, right, rows, dims):
    high, low = split(right)
    both = lax.dot_general(left[...], high, dims, preferred_element_type=jnp.float32)
    cross = lax.dot_general(left[:rows], low, dims, preferred_element_type=jnp.float32)
    return both[:rows] + (both[rows:] + cross)


def first_kernel(near_ref, far_ref, own_ref, sib_ref, out_ref, parts):
    half = near_ref.shape[0]
    rows = 2 * half

    @pl.when(pl.program_id(0) == 0)
    def _():
        parts[:half], parts[rows : rows + half] = split(near_ref[...])
        parts[half:rows], parts[rows + half :] = split(far_ref[...])

    tile = own_ref.shape[0]
    rows_of_h = jnp.concatenate([own_ref[...], sib_ref[...]], axis=0)
    product = dot_f32(parts, rows_of_h, rows, (((1,), (1,)), ((), ())))
    for which in range(2):
        out_ref[which] = -step_size * product[:, which * tile : (which + 1) * tile]


def first(near, far, own, sib):
    half, depth = near.shape
    rows = own.shape[0]
    tile = 128 if rows % 128 == 0 else rows
    whole = pl.BlockSpec((half, depth), lambda i: (0, 0))
    band = pl.BlockSpec((tile, depth), lambda i: (i, 0))
    return pl.pallas_call(
        first_kernel,
        grid=(rows // tile,),
        in_specs=[whole, whole, band, band],
        out_specs=pl.BlockSpec((2, 2 * half, tile), lambda i: (0, 0, i)),
        out_shape=jax.ShapeDtypeStruct((2, 2 * half, rows), jnp.float32),
        scratch_shapes=[pltpu.VMEM((4 * half, depth), jnp.bfloat16)],
        compiler_params=pltpu.CompilerParams(vmem_limit_bytes=VMEM_BYTES),
        cost_estimate=pl.CostEstimate(
            flops=3 * 2 * 4 * half * depth * rows, bytes_accessed=8 * rows * depth, transcendentals=0
        ),
        name="first_product",
    )(near, far, own, sib)


def second_kernel(change_ref, own_ref, sib_ref, near_ref, far_ref, parts):
    _, rows, depth = change_ref.shape
    half = rows // 2

    @pl.when(pl.program_id(0) == 0)
    def _():
        for which in range(2):
            places = slice(which * depth, (which + 1) * depth)
            parts[:rows, places], parts[rows:, places] = split(change_ref[which])

    rows_of_h = jnp.concatenate([own_ref[...], sib_ref[...]], axis=0)
    product = dot_f32(parts, rows_of_h, rows, (((1,), (0,)), ((), ())))
    near_ref[...] = product[:half]
    far_ref[...] = product[half:]


def second(change, own, sib):
    _, rows, depth = change.shape
    half = rows // 2
    columns = own.shape[1]
    tile = next((t for t in (512, 256, 128) if columns % t == 0), columns)
    band = pl.BlockSpec((depth, tile), lambda i: (0, i))
    out = pl.BlockSpec((half, tile), lambda i: (0, i))
    return pl.pallas_call(
        second_kernel,
        grid=(columns // tile,),
        in_specs=[pl.BlockSpec((2, rows, depth), lambda i: (0, 0, 0)), band, band],
        out_specs=[out, out],
        out_shape=[jax.ShapeDtypeStruct((half, columns), jnp.float32)] * 2,
        scratch_shapes=[pltpu.VMEM((2 * rows, 2 * depth), jnp.bfloat16)],
        compiler_params=pltpu.CompilerParams(vmem_limit_bytes=VMEM_BYTES),
        cost_estimate=pl.CostEstimate(
            flops=3 * 2 * 2 * rows * depth * columns, bytes_accessed=8 * depth * columns, transcendentals=0
        ),
        name="second_product",
    )(change, own, sib)


def per_device(rows_of, planes, hessian, dense_weight, start_iterate, start_multiplier, keep_mask):
    ring = rows_of // (CORES * PAIR)
    chips = ring * PAIR
    per_plane = chips // planes
    depth, columns = hessian.shape
    half = dense_weight.shape[1]
    row = lax.axis_index("row")
    plane = lax.axis_index("col")
    core = row % CORES
    pair = (row // CORES) % PAIR
    place = row // (CORES * PAIR)

    def device(z, x, c):
        return ((z % ring) * PAIR + x) * CORES + c

    everyone = [(z, x, c) for z in range(ring) for x in range(PAIR) for c in range(CORES)]
    to_sibling = [(device(z, x, c), device(z, x, 1 - c)) for z, x, c in everyone]
    to_pair = [(device(z, x, c), device(z, x ^ 1, c)) for z, x, c in everyone]
    to_next = [(device(z, x, c), device(z + 1, x, c)) for z, x, c in everyone]

    def route(shift, flip):
        turn = cross(shift, flip)
        pairs = []
        for z, x, c in everyone:
            for y in range(planes):
                chip = ((z + shift) % ring) * PAIR + (x ^ flip)
                if chip // per_plane == (y - turn) % planes:
                    pairs.append((device(z, x, c) * planes + y, device(z + shift, x ^ flip, c) * planes + y))
        return pairs

    def route_back(shift, flip):
        turn = cross(shift, flip)
        return [(b, a - a % planes + (a - turn) % planes) for a, b in route(shift, flip)]

    def cross(shift, flip):
        return 1 if shift and flip else 0

    both = ("row", "col")
    permute = lax.ppermute

    dense, begun, dual = dense_weight.T, start_iterate.T, start_multiplier.T
    keeping = keep_mask.T.astype(jnp.float32)
    change = begun - dense
    sibling = permute(hessian, "row", to_sibling)
    rest = begun - step_size * (penalty * (begun - keeping * (begun + dual) + dual)) - dense
    def piece(shift, flip):
        turn = cross(shift, flip)
        chip = ((place + shift) % ring) * PAIR + (pair ^ flip)
        at = jnp.clip(chip - ((plane - turn) % planes) * per_plane, 0, per_plane - 1)
        part = lax.dynamic_slice_in_dim(rest_by[turn], at * CORES * depth, CORES * depth, 1)
        part = part.reshape(half, CORES, depth)
        part = jnp.where(core == 0, part, part[:, ::-1]).transpose(1, 0, 2)
        if shift == 0 and flip == 0:
            return jnp.where(chip // per_plane == plane, part, 0.0)
        return permute(part, both, route(shift, flip))

    def sum_planes(part):
        others = [permute(part, "col", [(y, (y + turn) % planes) for y in range(planes)]) for turn in range(1, planes)]
        return functools.reduce(jnp.add, others) if others else jnp.zeros_like(part)

    rest_by = {0: rest}
    near, far, added = {0: change}, {}, {}
    product, mine, other, changed, kept, sent, swapped, back = {}, {}, {}, {}, {}, {}, {}, {}
    total = None
    start = max(ring, 4)
    returns = {group + 2: [(group, 0), (group, 1)] for group in range(1, ring)}
    returns.setdefault(start + ring - 2, []).extend([(0, 0), (0, 1)])
    for window in range(start + ring):
        fresh = []

        def put(where, key, value):
            where[key] = value
            fresh.append((where, key))

        if window < ring - 1:
            put(near, window + 1, permute(near[window], "row", to_next))
        if window < ring:
            put(far, window, permute(near[window], "row", to_pair))
        if window == 0:
            rest_by[1] = (permute(rest, "col", [(y, (y + 1) % planes) for y in range(planes)]))
        for group in (0, 1) if window == 1 else (window - 1,) if 2 < window <= ring else ():
            for flip in range(PAIR):
                added[group, flip] = piece(group, flip)
        if window == 2:
            fresh += [(added, (0, flip)) for flip in range(PAIR)]
        closing = window - start + 1
        if closing >= 1:
            if total is not None:
                total = permute(total, "row", to_next)
            put(swapped, closing % ring, permute(sent[closing % ring], "row", to_pair))
        def join(group):
            put(mine, group, product[group] + jnp.concatenate([added[group, 0], added[group, 1]], axis=1))
            other[group] = sum_planes(mine[group])

        group = window - 1
        if 0 <= group < ring:
            put(product, group, first(near[group], far[group], hessian, sibling))
            if group in (1, ring - 1):
                join(group)
        if window == start + 1:
            join(0)
        group = 0 if window == start + ring - 2 else window - 2
        if 1 <= group < ring or window == start + ring - 2:
            if 2 <= group < ring - 1:
                product[group + 1], other[group] = lax.optimization_barrier((product[group + 1], other[group]))
            put(changed, group, mine[group] + other[group])
            keep, send = second(changed[group], hessian, sibling)
            if 2 <= window - 1 < ring - 1:
                keep, product[window - 1] = lax.optimization_barrier((keep, product[window - 1]))
                join(window - 1)
            put(kept, group, keep)
            put(sent, group, send)
        for group, flip in returns.get(window, []):
            rows = changed[group][:, flip * half : (flip + 1) * half]
            put(back, (group, flip), permute(rows, both, route_back(group, flip)) if group or flip else rows)
        values = [where[key] for where, key in fresh]
        values, sibling, total, rest_by = lax.optimization_barrier((values, sibling, total, rest_by))
        for (where, key), value in zip(fresh, values):
            where[key] = value
        if closing >= 1:
            part = kept[closing % ring] + swapped[closing % ring]
            total = part if total is None else total + part
    gradient = total

    back = jnp.stack([back[shift, flip] for shift in range(ring) for flip in range(PAIR)])
    blocks = []
    for block in range(per_plane):
        chip = plane * per_plane + block
        slot = ((chip // PAIR - place) % ring) * PAIR + ((chip % PAIR) ^ pair)
        part = lax.dynamic_index_in_dim(back, slot, 0, keepdims=False)
        part = jnp.where(core == 0, part, part[::-1])
        blocks += [part[0], part[1]]
    iterate = jnp.concatenate(blocks, axis=1) + dense

    projected = keeping * (iterate + dual)
    multiplier = dual + iterate - projected
    iterate = iterate - step_size * (gradient + penalty * (iterate - projected + multiplier))
    projected = keeping * (iterate + multiplier)
    multiplier = multiplier + iterate - projected
    return (iterate.T, projected.T, multiplier.T)


def solution(mesh):
    return jax.shard_map(
        functools.partial(per_device, mesh.shape["row"], mesh.shape["col"]),
        mesh=mesh,
        in_specs=(
            P("row", "col"),
            P("col", "row"),
            P("col", "row"),
            P("col", "row"),
            P("col", "row"),
        ),
        out_specs=(P("col", "row"), P("col", "row"), P("col", "row")),
        check_vma=False,
    )
```

```python
import functools

import jax
import jax.numpy as jnp
from jax import lax
from jax.experimental import pallas as pl
from jax.experimental.pallas import tpu as pltpu
from jax.sharding import PartitionSpec as P

step_size = 0.25
penalty = 1.0

CORES = 2
PAIR = 2
VMEM_BYTES = 48 * 1024 * 1024


def split(value):
    high = value.astype(jnp.bfloat16)
    low = (value - high.astype(jnp.float32)).astype(jnp.bfloat16)
    return high, low


def dot_f32(left, right, rows, dims):
    high, low = split(right)
    both = lax.dot_general(left[...], high, dims, preferred_element_type=jnp.float32)
    cross = lax.dot_general(left[:rows], low, dims, preferred_element_type=jnp.float32)
    return both[:rows] + (both[rows:] + cross)


def first_kernel(near_ref, far_ref, own_ref, sib_ref, out_ref, parts):
    half = near_ref.shape[0]
    rows = 2 * half

    @pl.when(pl.program_id(0) == 0)
    def _():
        parts[:half], parts[rows : rows + half] = split(near_ref[...])
        parts[half:rows], parts[rows + half :] = split(far_ref[...])

    tile = own_ref.shape[0]
    rows_of_h = jnp.concatenate([own_ref[...], sib_ref[...]], axis=0)
    product = dot_f32(parts, rows_of_h, rows, (((1,), (1,)), ((), ())))
    for which in range(2):
        out_ref[which] = -step_size * product[:, which * tile : (which + 1) * tile]


def first(near, far, own, sib):
    half, depth = near.shape
    rows = own.shape[0]
    tile = 128 if rows % 128 == 0 else rows
    whole = pl.BlockSpec((half, depth), lambda i: (0, 0))
    band = pl.BlockSpec((tile, depth), lambda i: (i, 0))
    return pl.pallas_call(
        first_kernel,
        grid=(rows // tile,),
        in_specs=[whole, whole, band, band],
        out_specs=pl.BlockSpec((2, 2 * half, tile), lambda i: (0, 0, i)),
        out_shape=jax.ShapeDtypeStruct((2, 2 * half, rows), jnp.float32),
        scratch_shapes=[pltpu.VMEM((4 * half, depth), jnp.bfloat16)],
        compiler_params=pltpu.CompilerParams(vmem_limit_bytes=VMEM_BYTES),
        cost_estimate=pl.CostEstimate(
            flops=3 * 2 * 4 * half * depth * rows, bytes_accessed=8 * rows * depth, transcendentals=0
        ),
        name="first_product",
    )(near, far, own, sib)


def second_kernel(change_ref, own_ref, sib_ref, near_ref, far_ref, parts):
    _, rows, depth = change_ref.shape
    half = rows // 2

    @pl.when(pl.program_id(0) == 0)
    def _():
        for which in range(2):
            places = slice(which * depth, (which + 1) * depth)
            parts[:rows, places], parts[rows:, places] = split(change_ref[which])

    rows_of_h = jnp.concatenate([own_ref[...], sib_ref[...]], axis=0)
    product = dot_f32(parts, rows_of_h, rows, (((1,), (0,)), ((), ())))
    near_ref[...] = product[:half]
    far_ref[...] = product[half:]


def second(change, own, sib):
    _, rows, depth = change.shape
    half = rows // 2
    columns = own.shape[1]
    tile = next((t for t in (512, 256, 128) if columns % t == 0), columns)
    band = pl.BlockSpec((depth, tile), lambda i: (0, i))
    out = pl.BlockSpec((half, tile), lambda i: (0, i))
    return pl.pallas_call(
        second_kernel,
        grid=(columns // tile,),
        in_specs=[pl.BlockSpec((2, rows, depth), lambda i: (0, 0, 0)), band, band],
        out_specs=[out, out],
        out_shape=[jax.ShapeDtypeStruct((half, columns), jnp.float32)] * 2,
        scratch_shapes=[pltpu.VMEM((2 * rows, 2 * depth), jnp.bfloat16)],
        compiler_params=pltpu.CompilerParams(vmem_limit_bytes=VMEM_BYTES),
        cost_estimate=pl.CostEstimate(
            flops=3 * 2 * 2 * rows * depth * columns, bytes_accessed=8 * depth * columns, transcendentals=0
        ),
        name="second_product",
    )(change, own, sib)


def per_device(rows_of, planes, hessian, dense_weight, start_iterate, start_multiplier, keep_mask):
    ring = rows_of // (CORES * PAIR)
    chips = ring * PAIR
    per_plane = chips // planes
    depth, columns = hessian.shape
    half = dense_weight.shape[1]
    row = lax.axis_index("row")
    plane = lax.axis_index("col")
    core = row % CORES
    pair = (row // CORES) % PAIR
    place = row // (CORES * PAIR)

    def device(z, x, c):
        return ((z % ring) * PAIR + x) * CORES + c

    everyone = [(z, x, c) for z in range(ring) for x in range(PAIR) for c in range(CORES)]
    to_sibling = [(device(z, x, c), device(z, x, 1 - c)) for z, x, c in everyone]
    to_pair = [(device(z, x, c), device(z, x ^ 1, c)) for z, x, c in everyone]
    to_next = [(device(z, x, c), device(z + 1, x, c)) for z, x, c in everyone]

    def route(shift, flip):
        turn = cross(shift, flip)
        pairs = []
        for z, x, c in everyone:
            for y in range(planes):
                chip = ((z + shift) % ring) * PAIR + (x ^ flip)
                if chip // per_plane == (y - turn) % planes:
                    pairs.append((device(z, x, c) * planes + y, device(z + shift, x ^ flip, c) * planes + y))
        return pairs

    def route_back(shift, flip):
        turn = cross(shift, flip)
        return [(b, a - a % planes + (a - turn) % planes) for a, b in route(shift, flip)]

    def cross(shift, flip):
        return 1 if shift and flip else 0

    both = ("row", "col")
    permute = lax.ppermute

    dense, begun, dual = dense_weight.T, start_iterate.T, start_multiplier.T
    keeping = keep_mask.T.astype(jnp.float32)
    change = begun - dense
    sibling = permute(hessian, "row", to_sibling)
    rest = begun - step_size * (penalty * (begun - keeping * (begun + dual) + dual)) - dense
    def piece(shift, flip):
        turn = cross(shift, flip)
        chip = ((place + shift) % ring) * PAIR + (pair ^ flip)
        at = jnp.clip(chip - ((plane - turn) % planes) * per_plane, 0, per_plane - 1)
        part = lax.dynamic_slice_in_dim(rest_by[turn], at * CORES * depth, CORES * depth, 1)
        part = part.reshape(half, CORES, depth)
        part = jnp.where(core == 0, part, part[:, ::-1]).transpose(1, 0, 2)
        if shift == 0 and flip == 0:
            return jnp.where(chip // per_plane == plane, part, 0.0)
        return permute(part, both, route(shift, flip))

    def sum_planes(part):
        others = [permute(part, "col", [(y, (y + turn) % planes) for y in range(planes)]) for turn in range(1, planes)]
        return functools.reduce(jnp.add, others) if others else jnp.zeros_like(part)

    rest_by = {0: rest}
    near, far, added = {0: change}, {}, {}
    product, mine, other, changed, kept, sent, swapped, back = {}, {}, {}, {}, {}, {}, {}, {}
    total = None
    start = max(ring, 4)
    returns = {group + 2: [(group, 0), (group, 1)] for group in range(1, ring)}
    returns.setdefault(start + 1, []).extend([(0, 0), (0, 1)])
    for window in range(start + ring):
        fresh = []

        def put(where, key, value):
            where[key] = value
            fresh.append((where, key))

        if window < ring - 1:
            put(near, window + 1, permute(near[window], "row", to_next))
        if window < ring:
            put(far, window, permute(near[window], "row", to_pair))
        if window == 0:
            rest_by[1] = (permute(rest, "col", [(y, (y + 1) % planes) for y in range(planes)]))
        for group in (0, 1) if window == 1 else (window - 1,) if 2 < window <= ring else ():
            for flip in range(PAIR):
                added[group, flip] = piece(group, flip)
        if window == 1:
            fresh += [(added, (group, flip)) for group in (0, 1) for flip in range(PAIR)]
        closing = window - start + 1
        if closing >= 1:
            if total is not None:
                total = permute(total, "row", to_next)
            put(swapped, closing % ring, permute(sent[closing % ring], "row", to_pair))
        def join(group):
            put(mine, group, product[group] + jnp.concatenate([added[group, 0], added[group, 1]], axis=1))
            other[group] = sum_planes(mine[group])

        group = window - 1
        if 0 <= group < ring:
            put(product, group, first(near[group], far[group], hessian, sibling))
            if group in (1, ring - 1):
                join(group)
        if window == 2:
            join(0)
        if window == 3:
            put(changed, 0, mine[0] + other[0])
        group = 0 if window == start + ring - 2 else window - 2
        if 1 <= group < ring or window == start + ring - 2:
            if 2 <= group < ring - 1:
                product[group + 1], other[group] = lax.optimization_barrier((product[group + 1], other[group]))
            if group:
                put(changed, group, mine[group] + other[group])
            keep, send = second(changed[group], hessian, sibling)
            if 2 <= window - 1 < ring - 1:
                keep, product[window - 1] = lax.optimization_barrier((keep, product[window - 1]))
                join(window - 1)
            put(kept, group, keep)
            put(sent, group, send)
        for group, flip in returns.get(window, []):
            rows = changed[group][:, flip * half : (flip + 1) * half]
            put(back, (group, flip), permute(rows, both, route_back(group, flip)) if group or flip else rows)
        values = [where[key] for where, key in fresh]
        values, sibling, total, rest_by = lax.optimization_barrier((values, sibling, total, rest_by))
        for (where, key), value in zip(fresh, values):
            where[key] = value
        if closing >= 1:
            part = kept[closing % ring] + swapped[closing % ring]
            total = part if total is None else total + part
    gradient = total

    back = jnp.stack([back[shift, flip] for shift in range(ring) for flip in range(PAIR)])
    blocks = []
    for block in range(per_plane):
        chip = plane * per_plane + block
        slot = ((chip // PAIR - place) % ring) * PAIR + ((chip % PAIR) ^ pair)
        part = lax.dynamic_index_in_dim(back, slot, 0, keepdims=False)
        part = jnp.where(core == 0, part, part[::-1])
        blocks += [part[0], part[1]]
    iterate = jnp.concatenate(blocks, axis=1) + dense

    projected = keeping * (iterate + dual)
    multiplier = dual + iterate - projected
    iterate = iterate - step_size * (gradient + penalty * (iterate - projected + multiplier))
    projected = keeping * (iterate + multiplier)
    multiplier = multiplier + iterate - projected
    return (iterate.T, projected.T, multiplier.T)


def solution(mesh):
    return jax.shard_map(
        functools.partial(per_device, mesh.shape["row"], mesh.shape["col"]),
        mesh=mesh,
        in_specs=(
            P("row", "col"),
            P("col", "row"),
            P("col", "row"),
            P("col", "row"),
            P("col", "row"),
        ),
        out_specs=(P("col", "row"), P("col", "row"), P("col", "row")),
        check_vma=False,
    )
```

```python
import functools

import jax
import jax.numpy as jnp
from jax import lax
from jax.experimental import pallas as pl
from jax.experimental.pallas import tpu as pltpu
from jax.sharding import PartitionSpec as P

step_size = 0.25
penalty = 1.0

CORES = 2
PAIR = 2
VMEM_BYTES = 48 * 1024 * 1024


def split(value):
    high = value.astype(jnp.bfloat16)
    low = (value - high.astype(jnp.float32)).astype(jnp.bfloat16)
    return high, low


def dot_f32(left, right, rows, dims):
    high, low = split(right)
    both = lax.dot_general(left[...], high, dims, preferred_element_type=jnp.float32)
    cross = lax.dot_general(left[:rows], low, dims, preferred_element_type=jnp.float32)
    return both[:rows] + (both[rows:] + cross)


def first_kernel(near_ref, far_ref, own_ref, sib_ref, out_ref, parts):
    half = near_ref.shape[0]
    rows = 2 * half

    @pl.when(pl.program_id(0) == 0)
    def _():
        parts[:half], parts[rows : rows + half] = split(near_ref[...])
        parts[half:rows], parts[rows + half :] = split(far_ref[...])

    tile = own_ref.shape[0]
    rows_of_h = jnp.concatenate([own_ref[...], sib_ref[...]], axis=0)
    product = dot_f32(parts, rows_of_h, rows, (((1,), (1,)), ((), ())))
    for which in range(2):
        out_ref[which] = -step_size * product[:, which * tile : (which + 1) * tile]


def first(near, far, own, sib):
    half, depth = near.shape
    rows = own.shape[0]
    tile = 128 if rows % 128 == 0 else rows
    whole = pl.BlockSpec((half, depth), lambda i: (0, 0))
    band = pl.BlockSpec((tile, depth), lambda i: (i, 0))
    return pl.pallas_call(
        first_kernel,
        grid=(rows // tile,),
        in_specs=[whole, whole, band, band],
        out_specs=pl.BlockSpec((2, 2 * half, tile), lambda i: (0, 0, i)),
        out_shape=jax.ShapeDtypeStruct((2, 2 * half, rows), jnp.float32),
        scratch_shapes=[pltpu.VMEM((4 * half, depth), jnp.bfloat16)],
        compiler_params=pltpu.CompilerParams(vmem_limit_bytes=VMEM_BYTES),
        cost_estimate=pl.CostEstimate(
            flops=3 * 2 * 4 * half * depth * rows, bytes_accessed=8 * rows * depth, transcendentals=0
        ),
        name="first_product",
    )(near, far, own, sib)


def second_kernel(change_ref, own_ref, sib_ref, near_ref, far_ref, parts):
    _, rows, depth = change_ref.shape
    half = rows // 2

    @pl.when(pl.program_id(0) == 0)
    def _():
        for which in range(2):
            places = slice(which * depth, (which + 1) * depth)
            parts[:rows, places], parts[rows:, places] = split(change_ref[which])

    rows_of_h = jnp.concatenate([own_ref[...], sib_ref[...]], axis=0)
    product = dot_f32(parts, rows_of_h, rows, (((1,), (0,)), ((), ())))
    near_ref[...] = product[:half]
    far_ref[...] = product[half:]


def second(change, own, sib):
    _, rows, depth = change.shape
    half = rows // 2
    columns = own.shape[1]
    tile = next((t for t in (512, 256, 128) if columns % t == 0), columns)
    band = pl.BlockSpec((depth, tile), lambda i: (0, i))
    out = pl.BlockSpec((half, tile), lambda i: (0, i))
    return pl.pallas_call(
        second_kernel,
        grid=(columns // tile,),
        in_specs=[pl.BlockSpec((2, rows, depth), lambda i: (0, 0, 0)), band, band],
        out_specs=[out, out],
        out_shape=[jax.ShapeDtypeStruct((half, columns), jnp.float32)] * 2,
        scratch_shapes=[pltpu.VMEM((2 * rows, 2 * depth), jnp.bfloat16)],
        compiler_params=pltpu.CompilerParams(vmem_limit_bytes=VMEM_BYTES),
        cost_estimate=pl.CostEstimate(
            flops=2 * depth * columns, bytes_accessed=depth * columns // 4, transcendentals=0
        ),
        name="second_product",
    )(change, own, sib)


def per_device(rows_of, planes, hessian, dense_weight, start_iterate, start_multiplier, keep_mask):
    ring = rows_of // (CORES * PAIR)
    chips = ring * PAIR
    per_plane = chips // planes
    depth, columns = hessian.shape
    half = dense_weight.shape[1]
    row = lax.axis_index("row")
    plane = lax.axis_index("col")
    core = row % CORES
    pair = (row // CORES) % PAIR
    place = row // (CORES * PAIR)

    def device(z, x, c):
        return ((z % ring) * PAIR + x) * CORES + c

    everyone = [(z, x, c) for z in range(ring) for x in range(PAIR) for c in range(CORES)]
    to_sibling = [(device(z, x, c), device(z, x, 1 - c)) for z, x, c in everyone]
    to_pair = [(device(z, x, c), device(z, x ^ 1, c)) for z, x, c in everyone]
    to_next = [(device(z, x, c), device(z + 1, x, c)) for z, x, c in everyone]

    def route(shift, flip):
        turn = cross(shift, flip)
        pairs = []
        for z, x, c in everyone:
            for y in range(planes):
                chip = ((z + shift) % ring) * PAIR + (x ^ flip)
                if chip // per_plane == (y - turn) % planes:
                    pairs.append((device(z, x, c) * planes + y, device(z + shift, x ^ flip, c) * planes + y))
        return pairs

    def route_back(shift, flip):
        turn = cross(shift, flip)
        return [(b, a - a % planes + (a - turn) % planes) for a, b in route(shift, flip)]

    def cross(shift, flip):
        return 1 if shift and flip else 0

    both = ("row", "col")
    permute = lax.ppermute

    dense, begun, dual = dense_weight.T, start_iterate.T, start_multiplier.T
    keeping = keep_mask.T.astype(jnp.float32)
    change = begun - dense
    sibling = permute(hessian, "row", to_sibling)
    dual, keeping, change = lax.optimization_barrier((dual, keeping, change))
    rest = begun - step_size * (penalty * (begun - keeping * (begun + dual) + dual)) - dense
    def piece(shift, flip):
        turn = cross(shift, flip)
        chip = ((place + shift) % ring) * PAIR + (pair ^ flip)
        at = jnp.clip(chip - ((plane - turn) % planes) * per_plane, 0, per_plane - 1)
        part = lax.dynamic_slice_in_dim(rest_by[turn], at * CORES * depth, CORES * depth, 1)
        part = part.reshape(half, CORES, depth)
        part = jnp.where(core == 0, part, part[:, ::-1]).transpose(1, 0, 2)
        if shift == 0 and flip == 0:
            return jnp.where(chip // per_plane == plane, part, 0.0)
        return permute(part, both, route(shift, flip))

    def sum_planes(part):
        others = [permute(part, "col", [(y, (y + turn) % planes) for y in range(planes)]) for turn in range(1, planes)]
        return functools.reduce(jnp.add, others) if others else jnp.zeros_like(part)

    rest_by = {0: rest}
    near, far, added = {0: change}, {}, {}
    product, mine, other, changed, kept, sent, swapped, back = {}, {}, {}, {}, {}, {}, {}, {}
    total = None
    start = max(ring, 4)
    returns = {group + 2: [(group, 0), (group, 1)] for group in range(1, ring)}
    returns.setdefault(start + 1, []).extend([(0, 0), (0, 1)])
    for window in range(start + ring):
        fresh = []

        def put(where, key, value):
            where[key] = value
            fresh.append((where, key))

        if window < ring - 1:
            put(near, window + 1, permute(near[window], "row", to_next))
        if window < ring - 1:
            put(far, window, permute(near[window], "row", to_pair))
        elif window == ring - 1:
            by_ring = half * 3 // 8 // 8 * 8
            parts = {0: permute(near[window][by_ring:], "row", to_pair), 1: permute(far[window - 1][:by_ring], "row", to_next)}
            fresh += [(parts, 0), (parts, 1)]
        if window == 0:
            rest_by[1] = (permute(rest, "col", [(y, (y + 1) % planes) for y in range(planes)]))
        for group in (0, 1) if window == 1 else (window - 1,) if 2 < window <= ring else ():
            for flip in range(PAIR):
                added[group, flip] = piece(group, flip)
        if window == 1:
            fresh += [(added, (group, flip)) for group in (0, 1) for flip in range(PAIR)]
        closing = window - start + 1
        if closing >= 1:
            if total is not None:
                total = permute(total, "row", to_next)
            put(swapped, closing % ring, permute(sent[closing % ring], "row", to_pair))
        def join(group):
            put(mine, group, product[group] + jnp.concatenate([added[group, 0], added[group, 1]], axis=1))
            other[group] = sum_planes(mine[group])

        group = window - 1
        if 0 <= group < ring:
            if group == ring - 1:
                far[group] = jnp.concatenate([parts[1], parts[0]], axis=0)
            put(product, group, first(near[group], far[group], hessian, sibling))
            if group in (1, ring - 1):
                join(group)
        if window == 2:
            join(0)
            fresh.append((other, 0))
        if window == 3:
            put(changed, 0, mine[0] + other[0])
        group = 0 if window == start + ring - 2 else window - 2
        if 1 <= group < ring or window == start + ring - 2:
            if 1 <= group < ring - 1:
                product[group + 1], other[group] = lax.optimization_barrier((product[group + 1], other[group]))
            if group:
                put(changed, group, mine[group] + other[group])
            if window == ring:
                changed[group], mine[ring - 1] = lax.optimization_barrier((changed[group], mine[ring - 1]))
                put(other, ring - 1, sum_planes(mine[ring - 1]))
            keep, send = second(changed[group], hessian, sibling)
            if 2 <= window - 1 < ring - 1:
                keep, product[window - 1] = lax.optimization_barrier((keep, product[window - 1]))
                join(window - 1)
            put(kept, group, keep)
            put(sent, group, send)
        for group, flip in returns.get(window, []):
            rows = changed[group][:, flip * half : (flip + 1) * half]
            put(back, (group, flip), permute(rows, both, route_back(group, flip)) if group or flip else rows)
        values = [where[key] for where, key in fresh]
        held = rest_by if window else {0: rest_by[0]}
        values, sibling, total, held = lax.optimization_barrier((values, sibling, total, held))
        rest_by.update(held)
        for (where, key), value in zip(fresh, values):
            where[key] = value
        if closing >= 1:
            part = kept[closing % ring] + swapped[closing % ring]
            total = part if total is None else total + part
    gradient = total

    back = jnp.stack([back[shift, flip] for shift in range(ring) for flip in range(PAIR)])
    blocks = []
    for block in range(per_plane):
        chip = plane * per_plane + block
        slot = ((chip // PAIR - place) % ring) * PAIR + ((chip % PAIR) ^ pair)
        part = lax.dynamic_index_in_dim(back, slot, 0, keepdims=False)
        part = jnp.where(core == 0, part, part[::-1])
        blocks += [part[0], part[1]]
    iterate = jnp.concatenate(blocks, axis=1) + dense

    projected = keeping * (iterate + dual)
    multiplier = dual + iterate - projected
    iterate = iterate - step_size * (gradient + penalty * (iterate - projected + multiplier))
    projected = keeping * (iterate + multiplier)
    multiplier = multiplier + iterate - projected
    return (iterate.T, projected.T, multiplier.T)


def solution(mesh):
    return jax.shard_map(
        functools.partial(per_device, mesh.shape["row"], mesh.shape["col"]),
        mesh=mesh,
        in_specs=(
            P("row", "col"),
            P("col", "row"),
            P("col", "row"),
            P("col", "row"),
            P("col", "row"),
        ),
        out_specs=(P("col", "row"), P("col", "row"), P("col", "row")),
        check_vma=False,
    )
```

```python
import functools

import jax
import jax.numpy as jnp
from jax import lax
from jax.experimental import pallas as pl
from jax.experimental.pallas import tpu as pltpu
from jax.sharding import PartitionSpec as P

step_size = 0.25
penalty = 1.0

CORES = 2
PAIR = 2
VMEM_BYTES = 48 * 1024 * 1024


def split(value):
    high = value.astype(jnp.bfloat16)
    low = (value - high.astype(jnp.float32)).astype(jnp.bfloat16)
    return high, low


def dot_f32(left, right, rows, dims):
    high, low = split(right)
    both = lax.dot_general(left[...], high, dims, preferred_element_type=jnp.float32)
    cross = lax.dot_general(left[:rows], low, dims, preferred_element_type=jnp.float32)
    return both[:rows] + (both[rows:] + cross)


def first_kernel(near_ref, far_ref, own_ref, sib_ref, out_ref, parts):
    half = near_ref.shape[0]
    rows = 2 * half

    @pl.when(pl.program_id(0) == 0)
    def _():
        parts[:half], parts[rows : rows + half] = split(near_ref[...])
        parts[half:rows], parts[rows + half :] = split(far_ref[...])

    tile = own_ref.shape[0]
    rows_of_h = jnp.concatenate([own_ref[...], sib_ref[...]], axis=0)
    product = dot_f32(parts, rows_of_h, rows, (((1,), (1,)), ((), ())))
    for which in range(2):
        out_ref[which] = -step_size * product[:, which * tile : (which + 1) * tile]


def first(near, far, own, sib):
    half, depth = near.shape
    rows = own.shape[0]
    tile = 128 if rows % 128 == 0 else rows
    whole = pl.BlockSpec((half, depth), lambda i: (0, 0))
    band = pl.BlockSpec((tile, depth), lambda i: (i, 0))
    return pl.pallas_call(
        first_kernel,
        grid=(rows // tile,),
        in_specs=[whole, whole, band, band],
        out_specs=pl.BlockSpec((2, 2 * half, tile), lambda i: (0, 0, i)),
        out_shape=jax.ShapeDtypeStruct((2, 2 * half, rows), jnp.float32),
        scratch_shapes=[pltpu.VMEM((4 * half, depth), jnp.bfloat16)],
        compiler_params=pltpu.CompilerParams(vmem_limit_bytes=VMEM_BYTES),
        cost_estimate=pl.CostEstimate(
            flops=3 * 2 * 4 * half * depth * rows, bytes_accessed=8 * rows * depth, transcendentals=0
        ),
        name="first_product",
    )(near, far, own, sib)


def second_kernel(change_ref, own_ref, sib_ref, near_ref, far_ref, parts):
    _, rows, depth = change_ref.shape
    half = rows // 2

    @pl.when(pl.program_id(0) == 0)
    def _():
        for which in range(2):
            places = slice(which * depth, (which + 1) * depth)
            parts[:rows, places], parts[rows:, places] = split(change_ref[which])

    rows_of_h = jnp.concatenate([own_ref[...], sib_ref[...]], axis=0)
    product = dot_f32(parts, rows_of_h, rows, (((1,), (0,)), ((), ())))
    near_ref[...] = product[:half]
    far_ref[...] = product[half:]


def second(change, own, sib):
    _, rows, depth = change.shape
    half = rows // 2
    columns = own.shape[1]
    tile = next((t for t in (512, 256, 128) if columns % t == 0), columns)
    band = pl.BlockSpec((depth, tile), lambda i: (0, i))
    out = pl.BlockSpec((half, tile), lambda i: (0, i))
    return pl.pallas_call(
        second_kernel,
        grid=(columns // tile,),
        in_specs=[pl.BlockSpec((2, rows, depth), lambda i: (0, 0, 0)), band, band],
        out_specs=[out, out],
        out_shape=[jax.ShapeDtypeStruct((half, columns), jnp.float32)] * 2,
        scratch_shapes=[pltpu.VMEM((2 * rows, 2 * depth), jnp.bfloat16)],
        compiler_params=pltpu.CompilerParams(vmem_limit_bytes=VMEM_BYTES),
        cost_estimate=pl.CostEstimate(
            flops=3 * 2 * 2 * rows * depth * columns, bytes_accessed=8 * depth * columns, transcendentals=0
        ),
        name="second_product",
    )(change, own, sib)


def per_device(rows_of, planes, hessian, dense_weight, start_iterate, start_multiplier, keep_mask):
    ring = rows_of // (CORES * PAIR)
    chips = ring * PAIR
    per_plane = chips // planes
    depth, columns = hessian.shape
    half = dense_weight.shape[1]
    row = lax.axis_index("row")
    plane = lax.axis_index("col")
    core = row % CORES
    pair = (row // CORES) % PAIR
    place = row // (CORES * PAIR)

    def device(z, x, c):
        return ((z % ring) * PAIR + x) * CORES + c

    everyone = [(z, x, c) for z in range(ring) for x in range(PAIR) for c in range(CORES)]
    to_sibling = [(device(z, x, c), device(z, x, 1 - c)) for z, x, c in everyone]
    to_pair = [(device(z, x, c), device(z, x ^ 1, c)) for z, x, c in everyone]
    to_next = [(device(z, x, c), device(z + 1, x, c)) for z, x, c in everyone]

    def route(shift, flip):
        turn = cross(shift, flip)
        pairs = []
        for z, x, c in everyone:
            for y in range(planes):
                chip = ((z + shift) % ring) * PAIR + (x ^ flip)
                if chip // per_plane == (y - turn) % planes:
                    pairs.append((device(z, x, c) * planes + y, device(z + shift, x ^ flip, c) * planes + y))
        return pairs

    def route_back(shift, flip):
        turn = cross(shift, flip)
        return [(b, a - a % planes + (a - turn) % planes) for a, b in route(shift, flip)]

    def cross(shift, flip):
        return 1 if shift and flip else 0

    both = ("row", "col")
    permute = lax.ppermute

    dense, begun, dual = dense_weight.T, start_iterate.T, start_multiplier.T
    keeping = keep_mask.T.astype(jnp.float32)
    change = begun - dense
    sibling = permute(hessian, "row", to_sibling)
    rest = begun - step_size * (penalty * (begun - keeping * (begun + dual) + dual)) - dense
    def cut(source, shift, flip):
        chip = ((place + shift) % ring) * PAIR + (pair ^ flip)
        at = jnp.clip(chip - ((plane - cross(shift, flip)) % planes) * per_plane, 0, per_plane - 1)
        part = lax.dynamic_slice_in_dim(source, at * CORES * depth, CORES * depth, 1)
        part = part.reshape(half, CORES, depth)
        part = jnp.where(core == 0, part, part[:, ::-1]).transpose(1, 0, 2)
        return part if shift or flip else jnp.where(chip // per_plane == plane, part, 0.0)

    def piece(shift, flip):
        part = cuts[shift, flip]
        return permute(part, both, route(shift, flip)) if shift or flip else part

    def sum_planes(part):
        others = [permute(part, "col", [(y, (y + turn) % planes) for y in range(planes)]) for turn in range(1, planes)]
        return functools.reduce(jnp.add, others) if others else jnp.zeros_like(part)

    cuts = {}
    near, far, added = {0: change}, {}, {}
    product, mine, other, changed, kept, sent, swapped, back = {}, {}, {}, {}, {}, {}, {}, {}
    total = None
    start = max(ring, 4)
    returns = {group + 2: [(group, 0), (group, 1)] for group in range(2, ring)}
    returns.setdefault(3, []).append((1, 0))
    returns.setdefault(4, []).append((1, 1))
    returns.setdefault(start + 2, []).extend([(0, 0), (0, 1)])
    for window in range(start + ring):
        fresh = []

        def put(where, key, value):
            where[key] = value
            fresh.append((where, key))

        if window < ring - 1:
            put(near, window + 1, permute(near[window], "row", to_next))
        if window < ring:
            put(far, window, permute(near[window], "row", to_pair))
        if window == 0:
            rest_across = permute(rest, "col", [(y, (y + 1) % planes) for y in range(planes)])
            cuts.update({(shift, 0): cut(rest, shift, 0) for shift in range(ring)})
            cuts[0, 1] = cut(rest, 0, 1)
        if window == 1:
            cuts.update({(shift, 1): cut(rest_across, shift, 1) for shift in range(1, ring)})
        if 0 < window < ring:
            for flip in range(PAIR):
                added[window, flip] = piece(window, flip)
                if window == ring - 1:
                    fresh.append((added, (window, flip)))
                if window == 1:
                    added[0, flip] = piece(0, flip)
        closing = window - start + 1
        if closing >= 1:
            if total is not None:
                total = permute(total, "row", to_next)
            put(swapped, closing % ring, permute(sent[closing % ring], "row", to_pair))
        group = window - 2
        if 1 <= group < ring:
            put(changed, group, mine[group] + other[group])
        if window == 2:
            fresh += [(added, (0, flip)) for flip in range(PAIR)]
        if window == start + 1:
            put(mine, 0, product[0] + jnp.concatenate([added[0, 0], added[0, 1]], axis=1))
            put(other, 0, sum_planes(mine[0]))
        if window == start + 2:
            put(changed, 0, mine[0] + other[0])
        group = window - 1
        if 0 <= group < ring:
            put(product, group, first(near[group], far[group], hessian, sibling))
            if group:
                put(mine, group, product[group] + jnp.concatenate([added[group, 0], added[group, 1]], axis=1))
                put(other, group, sum_planes(mine[group]))
        group = 0 if window == start + ring - 2 else window - 2
        if 1 <= group < ring or window == start + ring - 2:
            keep, send = second(changed[group], hessian, sibling)
            put(kept, group, keep)
            put(sent, group, send)
        for group, flip in returns.get(window, []):
            rows = changed[group][:, flip * half : (flip + 1) * half]
            put(back, (group, flip), permute(rows, both, route_back(group, flip)) if group or flip else rows)
        values = [where[key] for where, key in fresh]
        waiting = {key: part for key, part in cuts.items() if key[0] > window or not window}
        values, sibling, total, waiting, rest_across = lax.optimization_barrier((values, sibling, total, waiting, rest_across))
        cuts.update(waiting)
        for (where, key), value in zip(fresh, values):
            where[key] = value
        if closing >= 1:
            part = kept[closing % ring] + swapped[closing % ring]
            total = part if total is None else total + part
    gradient = total

    back = jnp.stack([back[shift, flip] for shift in range(ring) for flip in range(PAIR)])
    blocks = []
    for block in range(per_plane):
        chip = plane * per_plane + block
        slot = ((chip // PAIR - place) % ring) * PAIR + ((chip % PAIR) ^ pair)
        part = lax.dynamic_index_in_dim(back, slot, 0, keepdims=False)
        part = jnp.where(core == 0, part, part[::-1])
        blocks += [part[0], part[1]]
    iterate = jnp.concatenate(blocks, axis=1) + dense

    projected = keeping * (iterate + dual)
    multiplier = dual + iterate - projected
    iterate = iterate - step_size * (gradient + penalty * (iterate - projected + multiplier))
    projected = keeping * (iterate + multiplier)
    multiplier = multiplier + iterate - projected
    return (iterate.T, projected.T, multiplier.T)


def solution(mesh):
    return jax.shard_map(
        functools.partial(per_device, mesh.shape["row"], mesh.shape["col"]),
        mesh=mesh,
        in_specs=(
            P("row", "col"),
            P("col", "row"),
            P("col", "row"),
            P("col", "row"),
            P("col", "row"),
        ),
        out_specs=(P("col", "row"), P("col", "row"), P("col", "row")),
        check_vma=False,
    )
```

```python
import functools

import jax
import jax.numpy as jnp
from jax import lax
from jax.experimental import pallas as pl
from jax.experimental.pallas import tpu as pltpu
from jax.sharding import PartitionSpec as P

step_size = 0.25
penalty = 1.0

CORES = 2
PAIR = 2
VMEM_BYTES = 48 * 1024 * 1024


def split(value):
    high = value.astype(jnp.bfloat16)
    low = (value - high.astype(jnp.float32)).astype(jnp.bfloat16)
    return high, low


def dot_f32(left, right, rows, dims):
    high, low = split(right)
    both = lax.dot_general(left[...], high, dims, preferred_element_type=jnp.float32)
    cross = lax.dot_general(left[:rows], low, dims, preferred_element_type=jnp.float32)
    return both[:rows] + (both[rows:] + cross)


def first_kernel(near_ref, far_ref, own_ref, sib_ref, out_ref, parts):
    half = near_ref.shape[0]
    rows = 2 * half

    @pl.when(pl.program_id(0) == 0)
    def _():
        parts[:half], parts[rows : rows + half] = split(near_ref[...])
        parts[half:rows], parts[rows + half :] = split(far_ref[...])

    tile = own_ref.shape[0]
    rows_of_h = jnp.concatenate([own_ref[...], sib_ref[...]], axis=0)
    product = dot_f32(parts, rows_of_h, rows, (((1,), (1,)), ((), ())))
    for which in range(2):
        out_ref[which] = -step_size * product[:, which * tile : (which + 1) * tile]


def first(near, far, own, sib):
    half, depth = near.shape
    rows = own.shape[0]
    tile = 128 if rows % 128 == 0 else rows
    whole = pl.BlockSpec((half, depth), lambda i: (0, 0))
    band = pl.BlockSpec((tile, depth), lambda i: (i, 0))
    return pl.pallas_call(
        first_kernel,
        grid=(rows // tile,),
        in_specs=[whole, whole, band, band],
        out_specs=pl.BlockSpec((2, 2 * half, tile), lambda i: (0, 0, i)),
        out_shape=jax.ShapeDtypeStruct((2, 2 * half, rows), jnp.float32),
        scratch_shapes=[pltpu.VMEM((4 * half, depth), jnp.bfloat16)],
        compiler_params=pltpu.CompilerParams(vmem_limit_bytes=VMEM_BYTES),
        cost_estimate=pl.CostEstimate(
            flops=3 * 2 * 4 * half * depth * rows, bytes_accessed=8 * rows * depth, transcendentals=0
        ),
        name="first_product",
    )(near, far, own, sib)


def second_kernel(change_ref, own_ref, sib_ref, near_ref, far_ref, parts):
    _, rows, depth = change_ref.shape
    half = rows // 2

    @pl.when(pl.program_id(0) == 0)
    def _():
        for which in range(2):
            places = slice(which * depth, (which + 1) * depth)
            parts[:rows, places], parts[rows:, places] = split(change_ref[which])

    rows_of_h = jnp.concatenate([own_ref[...], sib_ref[...]], axis=0)
    product = dot_f32(parts, rows_of_h, rows, (((1,), (0,)), ((), ())))
    near_ref[...] = product[:half]
    far_ref[...] = product[half:]


def second(change, own, sib):
    _, rows, depth = change.shape
    half = rows // 2
    columns = own.shape[1]
    tile = next((t for t in (512, 256, 128) if columns % t == 0), columns)
    band = pl.BlockSpec((depth, tile), lambda i: (0, i))
    out = pl.BlockSpec((half, tile), lambda i: (0, i))
    return pl.pallas_call(
        second_kernel,
        grid=(columns // tile,),
        in_specs=[pl.BlockSpec((2, rows, depth), lambda i: (0, 0, 0)), band, band],
        out_specs=[out, out],
        out_shape=[jax.ShapeDtypeStruct((half, columns), jnp.float32)] * 2,
        scratch_shapes=[pltpu.VMEM((2 * rows, 2 * depth), jnp.bfloat16)],
        compiler_params=pltpu.CompilerParams(vmem_limit_bytes=VMEM_BYTES),
        cost_estimate=pl.CostEstimate(
            flops=3 * 2 * 2 * rows * depth * columns, bytes_accessed=8 * depth * columns, transcendentals=0
        ),
        name="second_product",
    )(change, own, sib)


def per_device(rows_of, planes, hessian, dense_weight, start_iterate, start_multiplier, keep_mask):
    ring = rows_of // (CORES * PAIR)
    chips = ring * PAIR
    per_plane = chips // planes
    depth, columns = hessian.shape
    half = dense_weight.shape[1]
    row = lax.axis_index("row")
    plane = lax.axis_index("col")
    core = row % CORES
    pair = (row // CORES) % PAIR
    place = row // (CORES * PAIR)

    def device(z, x, c):
        return ((z % ring) * PAIR + x) * CORES + c

    everyone = [(z, x, c) for z in range(ring) for x in range(PAIR) for c in range(CORES)]
    to_sibling = [(device(z, x, c), device(z, x, 1 - c)) for z, x, c in everyone]
    to_pair = [(device(z, x, c), device(z, x ^ 1, c)) for z, x, c in everyone]
    to_next = [(device(z, x, c), device(z + 1, x, c)) for z, x, c in everyone]

    def route(shift, flip):
        turn = cross(shift, flip)
        pairs = []
        for z, x, c in everyone:
            for y in range(planes):
                chip = ((z + shift) % ring) * PAIR + (x ^ flip)
                if chip // per_plane == (y - turn) % planes:
                    pairs.append((device(z, x, c) * planes + y, device(z + shift, x ^ flip, c) * planes + y))
        return pairs

    def route_back(shift, flip):
        turn = cross(shift, flip)
        return [(b, a - a % planes + (a - turn) % planes) for a, b in route(shift, flip)]

    def cross(shift, flip):
        return 1 if shift and flip else 0

    both = ("row", "col")
    permute = lax.ppermute

    dense, begun, dual = dense_weight.T, start_iterate.T, start_multiplier.T
    keeping = keep_mask.T.astype(jnp.float32)
    change = begun - dense
    sibling = permute(hessian, "row", to_sibling)
    rest = begun - step_size * (penalty * (begun - keeping * (begun + dual) + dual)) - dense
    def cut(source, shift, flip):
        chip = ((place + shift) % ring) * PAIR + (pair ^ flip)
        at = jnp.clip(chip - ((plane - cross(shift, flip)) % planes) * per_plane, 0, per_plane - 1)
        part = lax.dynamic_slice_in_dim(source, at * CORES * depth, CORES * depth, 1)
        part = part.reshape(half, CORES, depth)
        part = jnp.where(core == 0, part, part[:, ::-1]).transpose(1, 0, 2)
        return part if shift or flip else jnp.where(chip // per_plane == plane, part, 0.0)

    def piece(shift, flip):
        part = cuts[shift, flip]
        return permute(part, both, route(shift, flip)) if shift or flip else part

    def sum_planes(part):
        others = [permute(part, "col", [(y, (y + turn) % planes) for y in range(planes)]) for turn in range(1, planes)]
        return functools.reduce(jnp.add, others) if others else jnp.zeros_like(part)

    cuts = {}
    near, far, added = {0: change}, {}, {}
    product, mine, other, changed, kept, sent, swapped, back = {}, {}, {}, {}, {}, {}, {}, {}
    total = None
    start = max(ring, 4)
    returns = {group + 2: [(group, 0), (group, 1)] for group in range(2, ring)}
    returns.setdefault(3, []).append((1, 0))
    returns.setdefault(4, []).append((1, 1))
    returns.setdefault(start + 2, []).extend([(0, 0), (0, 1)])
    for window in range(start + ring):
        fresh = []

        def put(where, key, value):
            where[key] = value
            fresh.append((where, key))

        if window < ring - 1:
            put(near, window + 1, permute(near[window], "row", to_next))
        if window < ring:
            put(far, window, permute(near[window], "row", to_pair))
        if window == 0:
            rest_across = permute(rest, "col", [(y, (y + 1) % planes) for y in range(planes)])
            cuts.update({(shift, 0): cut(rest, shift, 0) for shift in range(ring)})
            cuts[0, 1] = cut(rest, 0, 1)
        if window == 1:
            cuts.update({(shift, 1): cut(rest_across, shift, 1) for shift in range(1, ring)})
        if 0 < window < ring:
            if window > 2:
                added[window - 1, 0] = piece(window - 1, 0)
            for flip in range(PAIR):
                if flip == 0 and 2 <= window < ring - 1:
                    continue
                added[window, flip] = piece(window, flip)
                if window == ring - 1:
                    fresh.append((added, (window, flip)))
                if window == 1:
                    added[0, flip] = piece(0, flip)
        closing = window - start + 1
        if closing >= 1:
            if total is not None:
                total = permute(total, "row", to_next)
            put(swapped, closing % ring, permute(sent[closing % ring], "row", to_pair))
        group = window - 2
        if 1 <= group < ring:
            put(changed, group, mine[group] + other[group])
        if window == 2:
            fresh += [(added, (0, flip)) for flip in range(PAIR)]
        if window == start + 1:
            put(mine, 0, product[0] + jnp.concatenate([added[0, 0], added[0, 1]], axis=1))
            put(other, 0, sum_planes(mine[0]))
        if window == start + 2:
            put(changed, 0, mine[0] + other[0])
        group = window - 1
        if 0 <= group < ring:
            put(product, group, first(near[group], far[group], hessian, sibling))
            if group:
                put(mine, group, product[group] + jnp.concatenate([added[group, 0], added[group, 1]], axis=1))
                put(other, group, sum_planes(mine[group]))
        group = 0 if window == start + ring - 2 else window - 2
        if 1 <= group < ring or window == start + ring - 2:
            keep, send = second(changed[group], hessian, sibling)
            put(kept, group, keep)
            put(sent, group, send)
        for group, flip in returns.get(window, []):
            rows = changed[group][:, flip * half : (flip + 1) * half]
            put(back, (group, flip), permute(rows, both, route_back(group, flip)) if group or flip else rows)
        values = [where[key] for where, key in fresh]
        waiting = {key: part for key, part in cuts.items() if key[0] > window or not window or (key == (window, 0) and 2 <= window < ring - 1)}
        values, sibling, total, waiting, rest_across = lax.optimization_barrier((values, sibling, total, waiting, rest_across))
        cuts.update(waiting)
        for (where, key), value in zip(fresh, values):
            where[key] = value
        if closing >= 1:
            part = kept[closing % ring] + swapped[closing % ring]
            total = part if total is None else total + part
    gradient = total

    back = jnp.stack([back[shift, flip] for shift in range(ring) for flip in range(PAIR)])
    blocks = []
    for block in range(per_plane):
        chip = plane * per_plane + block
        slot = ((chip // PAIR - place) % ring) * PAIR + ((chip % PAIR) ^ pair)
        part = lax.dynamic_index_in_dim(back, slot, 0, keepdims=False)
        part = jnp.where(core == 0, part, part[::-1])
        blocks += [part[0], part[1]]
    iterate = jnp.concatenate(blocks, axis=1) + dense

    projected = keeping * (iterate + dual)
    multiplier = dual + iterate - projected
    iterate = iterate - step_size * (gradient + penalty * (iterate - projected + multiplier))
    projected = keeping * (iterate + multiplier)
    multiplier = multiplier + iterate - projected
    return (iterate.T, projected.T, multiplier.T)


def solution(mesh):
    return jax.shard_map(
        functools.partial(per_device, mesh.shape["row"], mesh.shape["col"]),
        mesh=mesh,
        in_specs=(
            P("row", "col"),
            P("col", "row"),
            P("col", "row"),
            P("col", "row"),
            P("col", "row"),
        ),
        out_specs=(P("col", "row"), P("col", "row"), P("col", "row")),
        check_vma=False,
    )
```

```python
import functools

import jax
import jax.numpy as jnp
from jax import lax
from jax.experimental import pallas as pl
from jax.experimental.pallas import tpu as pltpu
from jax.sharding import PartitionSpec as P

step_size = 0.25
penalty = 1.0

CORES = 2
PAIR = 2
VMEM_BYTES = 48 * 1024 * 1024


def split(value):
    high = value.astype(jnp.bfloat16)
    low = (value - high.astype(jnp.float32)).astype(jnp.bfloat16)
    return high, low


def dot_f32(left, right, rows, dims):
    high, low = split(right)
    both = lax.dot_general(left[...], high, dims, preferred_element_type=jnp.float32)
    cross = lax.dot_general(left[:rows], low, dims, preferred_element_type=jnp.float32)
    return both[:rows] + (both[rows:] + cross)


def first_kernel(near_ref, far_ref, own_ref, sib_ref, out_ref, parts):
    half = near_ref.shape[0]
    rows = 2 * half

    @pl.when(pl.program_id(0) == 0)
    def _():
        parts[:half], parts[rows : rows + half] = split(near_ref[...])
        parts[half:rows], parts[rows + half :] = split(far_ref[...])

    tile = own_ref.shape[0]
    rows_of_h = jnp.concatenate([own_ref[...], sib_ref[...]], axis=0)
    product = dot_f32(parts, rows_of_h, rows, (((1,), (1,)), ((), ())))
    for which in range(2):
        out_ref[which] = -step_size * product[:, which * tile : (which + 1) * tile]


def first(near, far, own, sib):
    half, depth = near.shape
    rows = own.shape[0]
    tile = 128 if rows % 128 == 0 else rows
    whole = pl.BlockSpec((half, depth), lambda i: (0, 0))
    band = pl.BlockSpec((tile, depth), lambda i: (i, 0))
    return pl.pallas_call(
        first_kernel,
        grid=(rows // tile,),
        in_specs=[whole, whole, band, band],
        out_specs=pl.BlockSpec((2, 2 * half, tile), lambda i: (0, 0, i)),
        out_shape=jax.ShapeDtypeStruct((2, 2 * half, rows), jnp.float32),
        scratch_shapes=[pltpu.VMEM((4 * half, depth), jnp.bfloat16)],
        compiler_params=pltpu.CompilerParams(vmem_limit_bytes=VMEM_BYTES),
        cost_estimate=pl.CostEstimate(
            flops=3 * 2 * 4 * half * depth * rows, bytes_accessed=8 * rows * depth, transcendentals=0
        ),
        name="first_product",
    )(near, far, own, sib)


def second_kernel(change_ref, own_ref, sib_ref, near_ref, far_ref, parts):
    _, rows, depth = change_ref.shape
    half = rows // 2

    @pl.when(pl.program_id(0) == 0)
    def _():
        for which in range(2):
            places = slice(which * depth, (which + 1) * depth)
            parts[:rows, places], parts[rows:, places] = split(change_ref[which])

    rows_of_h = jnp.concatenate([own_ref[...], sib_ref[...]], axis=0)
    product = dot_f32(parts, rows_of_h, rows, (((1,), (0,)), ((), ())))
    near_ref[...] = product[:half]
    far_ref[...] = product[half:]


def second(change, own, sib):
    _, rows, depth = change.shape
    half = rows // 2
    columns = own.shape[1]
    tile = next((t for t in (512, 256, 128) if columns % t == 0), columns)
    band = pl.BlockSpec((depth, tile), lambda i: (0, i))
    out = pl.BlockSpec((half, tile), lambda i: (0, i))
    return pl.pallas_call(
        second_kernel,
        grid=(columns // tile,),
        in_specs=[pl.BlockSpec((2, rows, depth), lambda i: (0, 0, 0)), band, band],
        out_specs=[out, out],
        out_shape=[jax.ShapeDtypeStruct((half, columns), jnp.float32)] * 2,
        scratch_shapes=[pltpu.VMEM((2 * rows, 2 * depth), jnp.bfloat16)],
        compiler_params=pltpu.CompilerParams(vmem_limit_bytes=VMEM_BYTES),
        cost_estimate=pl.CostEstimate(
            flops=3 * 2 * 2 * rows * depth * columns, bytes_accessed=8 * depth * columns, transcendentals=0
        ),
        name="second_product",
    )(change, own, sib)


def per_device(rows_of, planes, hessian, dense_weight, start_iterate, start_multiplier, keep_mask):
    ring = rows_of // (CORES * PAIR)
    chips = ring * PAIR
    per_plane = chips // planes
    depth, columns = hessian.shape
    half = dense_weight.shape[1]
    row = lax.axis_index("row")
    plane = lax.axis_index("col")
    core = row % CORES
    pair = (row // CORES) % PAIR
    place = row // (CORES * PAIR)

    def device(z, x, c):
        return ((z % ring) * PAIR + x) * CORES + c

    everyone = [(z, x, c) for z in range(ring) for x in range(PAIR) for c in range(CORES)]
    to_sibling = [(device(z, x, c), device(z, x, 1 - c)) for z, x, c in everyone]
    to_pair = [(device(z, x, c), device(z, x ^ 1, c)) for z, x, c in everyone]
    to_next = [(device(z, x, c), device(z + 1, x, c)) for z, x, c in everyone]

    def route(shift, flip):
        turn = cross(shift, flip)
        pairs = []
        for z, x, c in everyone:
            for y in range(planes):
                chip = ((z + shift) % ring) * PAIR + (x ^ flip)
                if chip // per_plane == (y - turn) % planes:
                    pairs.append((device(z, x, c) * planes + y, device(z + shift, x ^ flip, c) * planes + y))
        return pairs

    def route_back(shift, flip):
        turn = cross(shift, flip)
        return [(b, a - a % planes + (a - turn) % planes) for a, b in route(shift, flip)]

    def cross(shift, flip):
        return 1 if shift and flip else 0

    both = ("row", "col")
    permute = lax.ppermute

    dense, begun, dual = dense_weight.T, start_iterate.T, start_multiplier.T
    keeping = keep_mask.T.astype(jnp.float32)
    change = begun - dense
    sibling = permute(hessian, "row", to_sibling)
    rest = begun - step_size * (penalty * (begun - keeping * (begun + dual) + dual)) - dense
    def cut(source, shift, flip):
        chip = ((place + shift) % ring) * PAIR + (pair ^ flip)
        at = jnp.clip(chip - ((plane - cross(shift, flip)) % planes) * per_plane, 0, per_plane - 1)
        part = lax.dynamic_slice_in_dim(source, at * CORES * depth, CORES * depth, 1)
        part = part.reshape(half, CORES, depth)
        part = jnp.where(core == 0, part, part[:, ::-1]).transpose(1, 0, 2)
        return part if shift or flip else jnp.where(chip // per_plane == plane, part, 0.0)

    def piece(shift, flip):
        part = cuts[shift, flip]
        return permute(part, both, route(shift, flip)) if shift or flip else part

    def sum_planes(part):
        others = [permute(part, "col", [(y, (y + turn) % planes) for y in range(planes)]) for turn in range(1, planes)]
        return functools.reduce(jnp.add, others) if others else jnp.zeros_like(part)

    cuts = {}
    near, far, added = {0: change}, {}, {}
    product, mine, other, changed, kept, sent, swapped, back = {}, {}, {}, {}, {}, {}, {}, {}
    total = None
    start = max(ring, 4)
    returns = {group + 2: [(group, 0), (group, 1)] for group in range(2, ring)}
    returns.setdefault(3, []).append((1, 0))
    returns.setdefault(4, []).append((1, 1))
    returns.setdefault(start + ring - 1, []).extend([(0, 0), (0, 1)])
    for window in range(start + ring):
        fresh = []

        def put(where, key, value):
            where[key] = value
            fresh.append((where, key))

        if window < ring - 1:
            put(near, window + 1, permute(near[window], "row", to_next))
        if window < ring:
            put(far, window, permute(near[window], "row", to_pair))
        if window == 0:
            rest_across = permute(rest, "col", [(y, (y + 1) % planes) for y in range(planes)])
            cuts.update({(shift, 0): cut(rest, shift, 0) for shift in range(ring)})
            cuts[0, 1] = cut(rest, 0, 1)
        if window == 1:
            cuts.update({(shift, 1): cut(rest_across, shift, 1) for shift in range(1, ring)})
        if 0 < window < ring:
            for flip in range(PAIR):
                added[window, flip] = piece(window, flip)
                if window == ring - 1:
                    fresh.append((added, (window, flip)))
                if window == 1:
                    added[0, flip] = piece(0, flip)
        closing = window - start + 1
        if closing >= 1:
            if total is not None:
                total = permute(total, "row", to_next)
            put(swapped, closing % ring, permute(sent[closing % ring], "row", to_pair))
        group = window - 2
        if 1 <= group < ring:
            put(changed, group, mine[group] + other[group])
        if window == 2:
            fresh += [(added, (0, flip)) for flip in range(PAIR)]
        if window == start + 1:
            put(mine, 0, product[0] + jnp.concatenate([added[0, 0], added[0, 1]], axis=1))
            put(other, 0, sum_planes(mine[0]))
        if window == start + 2:
            put(changed, 0, mine[0] + other[0])
        group = window - 1
        if 0 <= group < ring:
            put(product, group, first(near[group], far[group], hessian, sibling))
            if group:
                put(mine, group, product[group] + jnp.concatenate([added[group, 0], added[group, 1]], axis=1))
                put(other, group, sum_planes(mine[group]))
        group = 0 if window == start + ring - 2 else window - 2
        if 1 <= group < ring or window == start + ring - 2:
            keep, send = second(changed[group], hessian, sibling)
            put(kept, group, keep)
            put(sent, group, send)
        for group, flip in returns.get(window, []):
            rows = changed[group][:, flip * half : (flip + 1) * half]
            put(back, (group, flip), permute(rows, both, route_back(group, flip)) if group or flip else rows)
        values = [where[key] for where, key in fresh]
        waiting = {key: part for key, part in cuts.items() if key[0] > window or not window}
        values, sibling, total, waiting, rest_across = lax.optimization_barrier((values, sibling, total, waiting, rest_across))
        cuts.update(waiting)
        for (where, key), value in zip(fresh, values):
            where[key] = value
        if closing >= 1:
            part = kept[closing % ring] + swapped[closing % ring]
            total = part if total is None else total + part
    gradient = total

    back = jnp.stack([back[shift, flip] for shift in range(ring) for flip in range(PAIR)])
    blocks = []
    for block in range(per_plane):
        chip = plane * per_plane + block
        slot = ((chip // PAIR - place) % ring) * PAIR + ((chip % PAIR) ^ pair)
        part = lax.dynamic_index_in_dim(back, slot, 0, keepdims=False)
        part = jnp.where(core == 0, part, part[::-1])
        blocks += [part[0], part[1]]
    iterate = jnp.concatenate(blocks, axis=1) + dense

    projected = keeping * (iterate + dual)
    multiplier = dual + iterate - projected
    iterate = iterate - step_size * (gradient + penalty * (iterate - projected + multiplier))
    projected = keeping * (iterate + multiplier)
    multiplier = multiplier + iterate - projected
    return (iterate.T, projected.T, multiplier.T)


def solution(mesh):
    return jax.shard_map(
        functools.partial(per_device, mesh.shape["row"], mesh.shape["col"]),
        mesh=mesh,
        in_specs=(
            P("row", "col"),
            P("col", "row"),
            P("col", "row"),
            P("col", "row"),
            P("col", "row"),
        ),
        out_specs=(P("col", "row"), P("col", "row"), P("col", "row")),
        check_vma=False,
    )
```
